512 devices in a mesh: blk: 128 (over z, y, core), term: 4 (over x).
Axes of the slice: x: 4, y: 4, z: 16, core: 2. Of those that a mesh axis runs over, the one named last changes fastest.
Arguments:
- psi: bfloat16 [512, 256, 256], P('blk'), may hold values from -6 to 6
- left_env: bfloat16 [8, 2, 256, 256], P('term'), may hold values from -0.25 to 0.25
- right_env: bfloat16 [8, 2, 256, 256], P('term'), may hold values from -0.25 to 0.25
- connect: int32 [8, 512], P('term'), may hold values from 0 to 511, each once within a row
- qclass: int32 [512], replicated, may hold values from 0 to 1
- sector_dims: int32 [512], replicated, may hold values from 64 to 256, as said below
Outputs:
- sigma_one: bfloat16 [512, 256, 256], P('blk')
- sigma_two: bfloat16 [512, 256, 256], P('term', 'blk')
The draws below stay inside these ranges and needn't reach their ends.
Inputs may be any that keep to these rules, and one draw needn't show every extreme that they name: `sector_dims`: some sector has dimension exactly 256 and some exactly 64. `connect`: each row is a permutation of the sectors.
All inputs are finite; a program needn't handle non-finite values.
Results may differ from the reference program's by a relative error of at most 0.0065.
Values may be sent and summed in bfloat16 or wider, within the bound.
No kernel may reach another device: no remote copies, remote signals or barrier semaphores. Data moves between devices by JAX's collectives and lax.ppermute only.
A program may use at most 64 MiB of HBM per device.

```python
import jax
import jax.numpy as jnp
from jax import lax

DS = 256
NQ = 2
NSEC = 512
NTERM = 8


def draw_sector_dims(key, part):
    key = jax.random.fold_in(key, 11)
    first, second = jax.random.split(key)
    dims = jax.random.randint(first, (NSEC,), DS // 4, DS + 1)
    place = jax.random.permutation(second, NSEC)
    where_line = jnp.arange(NSEC)
    dims = jnp.where(where_line == place[0], DS, dims)
    dims = jnp.where(where_line == place[1], DS // 4, dims)
    return dims.astype(jnp.int32)


def with_ends(entries, stream_key, least, top_value):
    longest = entries.shape.index(max(entries.shape))
    spots = []
    for shift in (0, 1):
        where = [jax.random.randint(jax.random.fold_in(stream_key, axis), (), 0, length) for axis, length in enumerate(entries.shape)]
        where[longest] = (where[longest] + shift) % entries.shape[longest]
        spots.append(tuple(where))
    return entries.at[spots[0]].set(least).at[spots[1]].set(top_value)


def block_levels(stream_key, shape, shards, least, largest):
    factor_of, own = 1.0, jax.random.fold_in(stream_key, 6)
    for position, blocks in shards:
        heights = jnp.exp(jax.random.uniform(jax.random.fold_in(own, position), (blocks,), jnp.float32, least / len(shards), largest / len(shards)))
        factor_of = factor_of * jnp.repeat(heights, shape[position] // blocks).reshape([-1 if axis == position else 1 for axis in range(len(shape))])
    return factor_of


def gaussian(stream_key, shape, deviation, bound, pieces=(), held_as=jnp.bfloat16):
    array = deviation * jax.random.normal(stream_key, shape, jnp.float32)
    if pieces:
        array = array * block_levels(stream_key, shape, pieces, -0.22, 0.18)
    return jnp.clip(array, -bound, bound).astype(held_as)


def setup_inputs(seed: int = 0) -> dict:
    key_list = jax.random.split(jax.random.key(seed), 7)
    return {
        "psi": gaussian(key_list[0], (NSEC, DS, DS), 1.0, 6.0, ((0, 128),)),
        "left_env": gaussian(key_list[1], (NTERM, NQ, DS, DS), (2 * DS) ** -0.5, 0.25, ((0, 4),)),
        "right_env": gaussian(key_list[2], (NTERM, NQ, DS, DS), (2 * DS) ** -0.5, 0.25, ((0, 4),)),
        "connect": jax.vmap(lambda own: jax.random.permutation(own, NSEC))(jax.random.split(key_list[3], NTERM)).reshape((NTERM, NSEC)).astype(jnp.int32),
        "qclass": with_ends(jax.random.randint(key_list[4], (NSEC,), 0, NQ), jax.random.fold_in(key_list[4], 1), 0, NQ - 1).astype(jnp.int32),
        "sector_dims": draw_sector_dims(jax.random.fold_in(key_list[6], 71), 0),
    }


def apply_h(vec, left_env, right_env, connect, qclass, mask):
    masked = vec.astype(jnp.float32) * mask

    def one_term(total, index):
        lsel = jnp.take(left_env[index], qclass, axis=0).astype(jnp.float32)
        contracted = jnp.einsum("sij,sjk->sik", lsel, masked).astype(jnp.bfloat16)
        source = jnp.take(contracted, connect[index], axis=0).astype(jnp.float32)
        rsel = jnp.take(right_env[index], qclass, axis=0).astype(jnp.float32)
        return total + jnp.einsum("sik,slk->sil", source, rsel), None

    start = jnp.zeros(vec.shape, jnp.float32)
    total, unused = lax.scan(one_term, start, jnp.arange(NTERM, dtype=jnp.int32))
    return (total * mask).astype(jnp.bfloat16)


def reference(psi, left_env, right_env, connect, qclass, sector_dims):
    line = jnp.arange(DS, dtype=jnp.int32)
    inside = (line[None, :, None] < sector_dims[:, None, None]) & (line[None, None, :] < sector_dims[:, None, None])
    mask = inside.astype(jnp.float32)
    sigma_one = apply_h(psi, left_env, right_env, connect, qclass, mask)
    sigma_two = apply_h(sigma_one, left_env, right_env, connect, qclass, mask)
    return sigma_one, sigma_two
```

```python
import jax
import jax.numpy as jnp
from jax import lax
from jax.experimental import pallas as pl
from jax.experimental.pallas import tpu as pltpu
from jax.sharding import PartitionSpec as P

LANES = 128


def pair_kernel(scalars, vec, left, right, order, out, wide):
    sec, width = vec.shape[0], vec.shape[1]
    terms, classes = left.shape[0], left.shape[1]
    half = width // 2
    pairs = terms * sec
    row = lax.broadcasted_iota(jnp.int32, (width, width), 0)
    col = lax.broadcasted_iota(jnp.int32, (width, width), 1)
    edge = jnp.maximum(row, col)
    for c in range(sec):
        masked = jnp.where(edge < scalars[sec + c], vec[c], jnp.zeros_like(vec[c]))
        for t in range(terms):
            contracted = jnp.dot(
                left[t, scalars[c]], masked, preferred_element_type=jnp.float32
            ).astype(jnp.bfloat16)
            sorted_rows = jnp.dot(
                order[...], contracted, preferred_element_type=jnp.float32
            ).astype(jnp.bfloat16)
            image = lax.dot_general(
                sorted_rows,
                right[t, scalars[2 * sec + t * sec + c]],
                (((1,), (1,)), ((), ())),
                preferred_element_type=jnp.float32,
            )
            pair = t * sec + c
            for j in range(wide.shape[0]):
                r, at = j // (width // LANES), j % (width // LANES) * LANES
                wide[j, pl.ds(pair, half, stride=pairs), :] = image[
                    r * half : (r + 1) * half, at : at + LANES
                ]
    for j in range(wide.shape[0]):
        out[:, j * LANES : (j + 1) * LANES] = wide[j].astype(jnp.bfloat16)


def pair_products(scalars, vec, left, right, order):
    terms, sec, width = left.shape[0], vec.shape[0], vec.shape[1]
    rows = terms * sec * width // 2
    vmem = pl.BlockSpec(memory_space=pltpu.VMEM)
    return pl.pallas_call(
        pair_kernel,
        out_shape=jax.ShapeDtypeStruct((rows, 2 * width), jnp.bfloat16),
        in_specs=[pl.BlockSpec(memory_space=pltpu.SMEM), vmem, vmem, vmem, vmem],
        out_specs=vmem,
        scratch_shapes=[pltpu.VMEM((2 * width // LANES, rows, LANES), jnp.float32)],
        compiler_params=pltpu.CompilerParams(vmem_limit_bytes=32 * 1024 * 1024),
        cost_estimate=pl.CostEstimate(
            flops=terms * sec * 3 * 2 * width**3, bytes_accessed=4 * 1024 * 1024, transcendentals=0
        ),
    )(scalars, vec, left, right, order)


def on_device(psi, left_env, right_env, connect, qclass, sector_dims):
    nblk = lax.axis_size("blk")
    nterm = lax.axis_size("term")
    sec_dev, width = psi.shape[0], psi.shape[1]
    band = width // nblk
    nsec = qclass.shape[0]
    terms = left_env.shape[0]
    pairs = terms * sec_dev
    blk = lax.axis_index("blk")
    first = blk * sec_dev

    mine = first + jnp.arange(sec_dev, dtype=jnp.int32)
    sectors = jnp.arange(nsec, dtype=jnp.int32)
    own = (sectors[None, :] == mine[:, None]).astype(jnp.int32)
    q_local = jnp.sum(own * qclass[None, :], axis=1)
    d_local = jnp.sum(own * sector_dims[None, :], axis=1)
    hit = (connect[:, None, :] == mine[None, :, None]).astype(jnp.int32)
    q_target = jnp.sum(hit * qclass[None, None, :], axis=2)
    scalars = jnp.concatenate([q_local, d_local, q_target.reshape(-1)])

    line = jnp.arange(width, dtype=jnp.int32)
    place = jnp.where(line < width // 2, 2 * line, 2 * line - width + 1)
    order = (place[:, None] == line[None, :]).astype(jnp.bfloat16)

    k = jnp.arange(nblk * pairs, dtype=jnp.int32)
    k_term = (k // sec_dev) % terms
    k_sector = (k // pairs) * sec_dev + k % sec_dev

    def routing(targets):
        wanted = jnp.zeros((nsec, k.shape[0]), jnp.int32)
        for t in range(terms):
            wanted = jnp.where(k_term[None, :] == t, targets[t][:, None], wanted)
        return (wanted == k_sector[None, :]).astype(jnp.bfloat16)

    def by_owner(a):
        return a.reshape(nblk, sec_dev).T.reshape(nsec)

    route_one = routing([by_owner(connect[t]) for t in range(terms)])
    route_two = routing([connect[t] for t in range(terms)])
    element = jnp.arange(band * width, dtype=jnp.int32)
    edge = jnp.maximum(blk * band + element // width, element % width)
    keep_one = edge[None, :] < by_owner(sector_dims)[:, None]
    keep_two = edge[None, :] < sector_dims[:, None]

    def product(vec, route, keep):
        sent = pair_products(scalars, vec, left_env, right_env, order)
        sent = sent.reshape(nblk, pairs, band * width)
        moved = lax.all_to_all(sent, "blk", split_axis=0, concat_axis=0, tiled=True)
        moved = moved.reshape(nblk * pairs, band * width)
        total = jnp.dot(route, moved, preferred_element_type=jnp.float32)
        total = jnp.where(keep, total, 0.0).astype(jnp.bfloat16)
        total = total.reshape(nterm, nsec // nterm, band * width)
        parts = lax.all_to_all(total, "term", split_axis=0, concat_axis=0, tiled=True)
        return jnp.sum(parts.astype(jnp.float32), axis=0).astype(jnp.bfloat16)

    one = product(psi, route_one, keep_one)
    one = one.reshape(nblk, band, width)
    one = lax.all_to_all(one, "blk", split_axis=0, concat_axis=0, tiled=True)
    one = one.reshape(1, width, width)
    sigma_one = lax.all_gather(one, "term", axis=0, tiled=True)
    two = product(sigma_one, route_two, keep_two)
    sigma_two = two.reshape(nsec // nterm, band, width)
    return (sigma_one, sigma_two)


def solution(mesh):
    placed = (
        P("blk", None, None),
        P("term", None, None, None),
        P("term", None, None, None),
        P("term", None),
        P(),
        P(),
    )
    return jax.shard_map(
        on_device,
        mesh=mesh,
        in_specs=placed,
        out_specs=(P("blk", None, None), P("term", "blk", None)),
        check_vma=False,
    )
```

```python
import functools

import jax
import jax.numpy as jnp
from jax import lax
from jax.experimental import pallas as pl
from jax.experimental.pallas import tpu as pltpu
from jax.sharding import PartitionSpec as P

LANES = 128
CODE_ROWS = 16
CODE_BASE = 16
F32, BF16 = jnp.float32, jnp.bfloat16
NT = (((1,), (1,)), ((), ()))


def matmul(a, b):
    return jnp.dot(a, b, preferred_element_type=F32)


def matmul_nt(a, b):
    return lax.dot_general(a, b, NT, preferred_element_type=F32)


def iota(shape, dim):
    return lax.broadcasted_iota(jnp.int32, shape, dim)


def split_order(width):
    half = width // 2
    line = iota((width, width), 0)
    place = jnp.where(line < half, 2 * line, 2 * line - width + 1)
    return (place == iota((width, width), 1)).astype(F32).astype(BF16)


def source_kernel(
    psi_hbm, left_hbm, right_hbm, conn_hbm, qclass_hbm, dims_hbm,
    out, left_out, right_out,
    psi, left, right, conn, qrow, qclass, dims, right_rows, code, wide, sems,
):
    sec, width = psi.shape[0], psi.shape[1]
    terms, classes = left.shape[0], left.shape[1]
    half, nsec = width // 2, conn.shape[1]
    pairs = (
        (right_hbm, right), (conn_hbm, conn), (left_hbm, left),
        (qclass_hbm, qclass), (qclass_hbm, qrow), (dims_hbm, dims), (psi_hbm, psi),
    )
    copies = [pltpu.make_async_copy(a, b, sems.at[i]) for i, (a, b) in enumerate(pairs)]
    for copy in copies:
        copy.start()
    order = split_order(width)
    edge = jnp.maximum(iota((width, width), 0), iota((width, width), 1))
    first = lax.axis_index("blk") * sec
    code[...] = jnp.zeros_like(code)
    copies[0].wait()
    for t in range(terms):
        for q in range(classes):
            right_rows[t, q] = matmul(order, right[t, q])
            right_out[t, q] = matmul_nt(right[t, q], order).astype(BF16)
    copies[1].wait()
    for t in range(terms):
        high = conn[t : t + 1, :] // CODE_BASE
        low = conn[t : t + 1, :] - high * CODE_BASE
        for j in range(nsec // width):
            code[pl.ds(j, 1), :] = high[:, j * width : (j + 1) * width].astype(F32)
            code[pl.ds(nsec // width + j, 1), :] = low[:, j * width : (j + 1) * width].astype(F32)
        left_out[t, classes * width :, :] = code[...].astype(BF16)
    copies[2].wait()
    for t in range(terms):
        for q in range(classes):
            left_out[t, q * width : (q + 1) * width, :] = matmul(order, left[t, q]).astype(BF16)
    for copy in copies[3:]:
        copy.wait()
    for c in range(sec):
        own = first + c
        masked = jnp.where(edge < dims[0, own], psi[c].astype(F32), 0.0).astype(BF16)
        target = jnp.sum(jnp.where(conn[...] == own, qrow[...].astype(F32), 0.0), axis=1, keepdims=True)
        for t in range(terms):
            contracted = matmul(left[t, qclass[0, own]], masked).astype(BF16)
            chosen = right_rows[t, 0]
            for q in range(1, classes):
                chosen = jnp.where(target[t : t + 1, :] == float(q), right_rows[t, q], chosen)
            image = matmul_nt(chosen.astype(BF16), contracted)
            pair = t * sec + c
            for j in range(wide.shape[0]):
                r, at = j // (width // LANES), j % (width // LANES) * LANES
                wide[j, pl.ds(pair, half, stride=terms * sec), :] = image[
                    r * half : (r + 1) * half, at : at + LANES
                ]
    for j in range(wide.shape[0]):
        out[:, j * LANES : (j + 1) * LANES] = wide[j].astype(BF16)


def gather_copies(sources, into, sems):
    each = into.shape[0] // len(sources)
    copies = [
        pltpu.make_async_copy(a, into.at[pl.ds(i * each, each)], sems.at[i])
        for i, a in enumerate(sources)
    ]
    for copy in copies:
        copy.start()
    return copies


def middle_kernel(classes, parts, qcol, *rest):
    sources, (out, left, wide, sems) = rest[:-4], rest[-4:]
    terms, nsec, width = left.shape[0], parts.shape[1], left.shape[2]
    half = width // 2
    copies = gather_copies(sources, left, sems)
    total = parts[0].astype(F32)
    for x in range(1, parts.shape[0]):
        total = total + parts[x].astype(F32)
    for j in range(total.shape[1] // LANES):
        wide[4, pl.ds(j, nsec, stride=terms), :] = total[:, j * LANES : (j + 1) * LANES]
    for j in range(total.shape[1] // LANES, terms):
        wide[4, pl.ds(j, nsec, stride=terms), :] = jnp.zeros((nsec, LANES), F32)
    chosen = []
    for q in range(classes):
        kept = jnp.where(qcol[...] == q, total, 0.0).astype(BF16)
        chosen.append(jnp.concatenate([kept[:, :width], kept[:, width:]], axis=0))
    for t in range(terms):
        if t % (terms // len(copies)) == 0:
            copies[t // (terms // len(copies))].wait()
        image = matmul_nt(left[t, 0:width, :], chosen[0])
        for q in range(1, classes):
            image = image + matmul_nt(left[t, q * width : (q + 1) * width, :], chosen[q])
        for j in range(4):
            ri, r = j // 2, j % 2
            wide[j, pl.ds(t, half, stride=terms), :] = image[
                ri * half : (ri + 1) * half, r * nsec : (r + 1) * nsec
            ]
    for j in range(5):
        out[:, j * LANES : (j + 1) * LANES] = wide[j].astype(BF16)


def target_kernel(spread, moved, conn, qrow, dims, *rest):
    sources, (out, right, wide, images, route, sector, sems) = rest[:-7], rest[-7:]
    terms, classes, width = right.shape[0], right.shape[1], right.shape[2]
    half, nsec = width // 2, conn.shape[1]
    blk, x = lax.axis_index("blk"), lax.axis_index("term")
    copies = gather_copies(sources, right, sems)
    for j in range(5):
        wide[j] = moved[:, j * LANES : (j + 1) * LANES].astype(F32)
    for ih in range(2):
        for r in range(2):
            sector[ih, pl.ds(r, half, stride=2), :] = wide[4, pl.ds(2 * r + ih, half, stride=terms), :]
    source = iota((LANES, nsec), 0) * spread + x
    for t in range(terms):
        route[t * LANES : (t + 1) * LANES, :] = (conn[t : t + 1, :] == source).astype(F32).astype(BF16)
    classes_row = jnp.broadcast_to(qrow[...].astype(F32), (8, nsec)).astype(BF16)
    target = matmul_nt(classes_row, route[...])
    for t in range(terms):
        if t % (terms // len(copies)) == 0:
            copies[t // (terms // len(copies))].wait()
        both = jnp.concatenate(
            [
                jnp.concatenate(
                    [wide[2 * ri + r, pl.ds(t, half, stride=terms), :] for r in range(2)], axis=0
                )
                for ri in range(2)
            ],
            axis=1,
        ).astype(BF16)
        pick = target[0:1, t * LANES : (t + 1) * LANES]
        pick = jnp.concatenate([pick, pick], axis=1)
        image = matmul(right[t, 0], both)
        for q in range(1, classes):
            image = jnp.where(pick == float(q), matmul(right[t, q], both), image)
        high = image.astype(BF16)
        low = (image - high.astype(F32)).astype(BF16)
        for ri in range(2):
            at = slice(t * LANES, (t + 1) * LANES)
            images[0, ri * width : (ri + 1) * width, at] = high[:, ri * LANES : (ri + 1) * LANES]
            images[1, ri * width : (ri + 1) * width, at] = low[:, ri * LANES : (ri + 1) * LANES]
    total = matmul(images[0], route[...]) + matmul(images[1], route[...])
    line = iota((2 * width, 1), 0)
    ri = (line >= width).astype(jnp.int32)
    edge = jnp.maximum(2 * blk + ri, line - ri * width)
    total = jnp.where(edge < dims[...], total, 0.0).astype(BF16)
    turned = [sector[ih].T.astype(BF16) for ih in range(2)]
    each = nsec // out.shape[0]
    for to in range(out.shape[0]):
        out[to, : 2 * width, :] = total[:, to * each : (to + 1) * each]
        for lh in range(2):
            for ih in range(2):
                first = 2 * width + lh * width + ih * LANES
                out[to, first : first + LANES, :] = turned[ih][:, lh * LANES : (lh + 1) * LANES]


def last_kernel(parts, one, two):
    width = one.shape[1]
    total = parts[0, : 2 * width, :].astype(F32)
    for x in range(1, parts.shape[0]):
        total = total + parts[x, : 2 * width, :].astype(F32)
    two[...] = total.T.astype(BF16)
    for x in range(parts.shape[0]):
        for lh in range(2):
            one[x, :, lh * LANES : (lh + 1) * LANES] = parts[
                x, (2 + lh) * width : (3 + lh) * width, :
            ]


def call(kernel, out_shape, in_specs, scratch, vmem_bytes, flops, *operands):
    vmem = pl.BlockSpec(memory_space=pltpu.VMEM)
    return pl.pallas_call(
        kernel,
        out_shape=out_shape,
        in_specs=in_specs,
        out_specs=jax.tree.map(lambda _: vmem, out_shape),
        scratch_shapes=scratch,
        compiler_params=pltpu.CompilerParams(vmem_limit_bytes=vmem_bytes),
        cost_estimate=pl.CostEstimate(flops=flops, bytes_accessed=6 << 20, transcendentals=0),
    )(*operands)


def from_all(a, axis):
    n = lax.axis_size(axis)
    return [a] + [lax.ppermute(a, axis, [(i, (i + d) % n) for i in range(n)]) for d in range(1, n)]


def on_device(psi, left_env, right_env, connect, qclass, sector_dims):
    nblk = lax.axis_size("blk")
    nterm = lax.axis_size("term")
    sec, width = psi.shape[0], psi.shape[1]
    band = width // nblk
    nsec = qclass.shape[0]
    terms, classes = left_env.shape[0], left_env.shape[1]
    pairs = terms * sec
    kept = nsec // nterm
    all_terms = terms * nterm
    blk = lax.axis_index("blk")
    x = lax.axis_index("term")
    vmem = pl.BlockSpec(memory_space=pltpu.VMEM)
    hbm = pl.BlockSpec(memory_space=pl.ANY)
    bf16 = lambda *shape: jax.ShapeDtypeStruct(shape, BF16)
    q_row, d_row = qclass[None, :], sector_dims[None, :]

    def by_owner(a):
        return a.reshape(nblk, sec).T.reshape(nsec)

    sent, left_mine, right_mine = call(
        source_kernel,
        (
            bf16(nblk * pairs, band * width),
            bf16(terms, classes * width + CODE_ROWS, width),
            bf16(terms, classes, width, width),
        ),
        [hbm] * 6,
        [
            pltpu.VMEM(psi.shape, BF16),
            pltpu.VMEM(left_env.shape, BF16),
            pltpu.VMEM(right_env.shape, BF16),
            pltpu.VMEM(connect.shape, jnp.int32),
            pltpu.VMEM(q_row.shape, jnp.int32),
            pltpu.SMEM(q_row.shape, jnp.int32),
            pltpu.SMEM(d_row.shape, jnp.int32),
            pltpu.VMEM(right_env.shape, F32),
            pltpu.VMEM((CODE_ROWS, width), F32),
            pltpu.VMEM((band * width // LANES, nblk * pairs, LANES), F32),
            pltpu.SemaphoreType.DMA((7,)),
        ],
        None,
        (2 * pairs + 3 * terms * classes) * 2 * width**3,
        psi, left_env, right_env, connect, q_row, d_row,
    )
    lefts = from_all(left_mine, "term")
    rights = from_all(right_mine, "term")
    code = jnp.concatenate([a[:, classes * width :, :] for a in lefts], axis=0).astype(F32)
    halves = nsec // width
    conn_all = CODE_BASE * code[:, :halves].reshape(all_terms, nsec) + code[
        :, halves : 2 * halves
    ].reshape(all_terms, nsec)
    conn_all = conn_all.astype(jnp.int32)

    k = jnp.arange(nblk * pairs, dtype=jnp.int32)
    k_term = (k // sec) % terms
    k_sector = (k // pairs) * sec + k % sec
    wanted = jnp.zeros((nsec, k.shape[0]), jnp.int32)
    for t in range(terms):
        wanted = jnp.where(k_term[None, :] == t, by_owner(connect[t])[:, None], wanted)
    route = (wanted == k_sector[None, :]).astype(BF16)
    element = jnp.arange(band * width, dtype=jnp.int32)
    edge = jnp.maximum(blk * band + element // width, element % width)
    keep = edge[None, :] < by_owner(sector_dims)[:, None]
    qcol = lax.dynamic_slice_in_dim(by_owner(qclass), x * kept, kept)[:, None]

    moved = lax.all_to_all(
        sent.reshape(nblk, pairs, band * width), "blk", split_axis=0, concat_axis=0, tiled=True
    ).reshape(nblk * pairs, band * width)
    total = jnp.where(keep, matmul(route, moved), 0.0).astype(BF16)
    parts = lax.all_to_all(
        total.reshape(nterm, kept, band * width), "term", split_axis=0, concat_axis=0, tiled=True
    )
    sent = call(
        functools.partial(middle_kernel, classes),
        bf16(nblk * all_terms, band * width + LANES),
        [vmem, vmem] + [hbm] * nterm,
        [
            pltpu.VMEM((all_terms,) + left_mine.shape[1:], BF16),
            pltpu.VMEM((5, nblk * all_terms, LANES), F32),
            pltpu.SemaphoreType.DMA((nterm,)),
        ],
        20 << 20,
        2 * all_terms * classes * width**3,
        parts, qcol, *lefts,
    )
    moved = lax.all_to_all(
        sent.reshape(nblk, all_terms, -1), "blk", split_axis=0, concat_axis=0, tiled=True
    ).reshape(nblk * all_terms, -1)
    sent = call(
        functools.partial(target_kernel, sec),
        bf16(nterm, 4 * width, kept),
        [vmem, vmem, vmem, vmem] + [hbm] * nterm,
        [
            pltpu.VMEM((all_terms,) + right_mine.shape[1:], BF16),
            pltpu.VMEM((5, nblk * all_terms, LANES), F32),
            pltpu.VMEM((2, band * width, all_terms * LANES), BF16),
            pltpu.VMEM((all_terms * LANES, nsec), BF16),
            pltpu.VMEM((2, width, LANES), F32),
            pltpu.SemaphoreType.DMA((nterm,)),
        ],
        28 << 20,
        2 * all_terms * (classes * width**3 + 2 * 2 * width * LANES * nsec),
        moved, conn_all, q_row, d_row, *rights,
    )
    parts = lax.all_to_all(sent, "term", split_axis=0, concat_axis=0, tiled=True)
    sigma_one, two = call(
        last_kernel,
        (bf16(sec, width, width), bf16(kept, band * width)),
        [vmem],
        [],
        16 << 20,
        0,
        parts,
    )
    return (sigma_one, two.reshape(kept, band, width))


def solution(mesh):
    placed = (
        P("blk", None, None),
        P("term", None, None, None),
        P("term", None, None, None),
        P("term", None),
        P(),
        P(),
    )
    return jax.shard_map(
        on_device,
        mesh=mesh,
        in_specs=placed,
        out_specs=(P("blk", None, None), P("term", "blk", None)),
        check_vma=False,
    )
```

```python
import functools

import jax
import jax.numpy as jnp
from jax import lax
from jax.experimental import pallas as pl
from jax.experimental.pallas import tpu as pltpu
from jax.sharding import PartitionSpec as P

LANES = 128
CODE_ROWS = 16
CODE_BASE = 16
F32, BF16 = jnp.float32, jnp.bfloat16
NT = (((1,), (1,)), ((), ()))


def matmul(a, b):
    return jnp.dot(a, b, preferred_element_type=F32)


def matmul_nt(a, b):
    return lax.dot_general(a, b, NT, preferred_element_type=F32)


def iota(shape, dim):
    return lax.broadcasted_iota(jnp.int32, shape, dim)


def split_order(width):
    half = width // 2
    line = iota((width, width), 0)
    place = jnp.where(line < half, 2 * line, 2 * line - width + 1)
    return (place == iota((width, width), 1)).astype(F32).astype(BF16)


def source_kernel(
    psi_hbm, left_hbm, right_hbm, conn_hbm, qclass_hbm, dims_hbm,
    out,
    psi, left, right, conn, qrow, qclass, dims, right_rows, wide, sems,
):
    sec, width = psi.shape[0], psi.shape[1]
    terms, classes = left.shape[0], left.shape[1]
    half = width // 2
    pairs = (
        (right_hbm, right), (conn_hbm, conn), (left_hbm, left),
        (qclass_hbm, qclass), (qclass_hbm, qrow), (dims_hbm, dims), (psi_hbm, psi),
    )
    copies = [pltpu.make_async_copy(a, b, sems.at[i]) for i, (a, b) in enumerate(pairs)]
    for copy in copies:
        copy.start()
    order = split_order(width)
    edge = jnp.maximum(iota((width, width), 0), iota((width, width), 1))
    first = lax.axis_index("blk") * sec
    copies[0].wait()
    for t in range(terms):
        for q in range(classes):
            right_rows[t, q] = matmul(order, right[t, q])
    for copy in copies[1:]:
        copy.wait()
    for c in range(sec):
        own = first + c
        masked = jnp.where(edge < dims[0, own], psi[c].astype(F32), 0.0).astype(BF16)
        target = jnp.sum(jnp.where(conn[...] == own, qrow[...].astype(F32), 0.0), axis=1, keepdims=True)
        for t in range(terms):
            contracted = matmul(left[t, qclass[0, own]], masked).astype(BF16)
            chosen = right_rows[t, 0]
            for q in range(1, classes):
                chosen = jnp.where(target[t : t + 1, :] == float(q), right_rows[t, q], chosen)
            image = matmul_nt(chosen.astype(BF16), contracted)
            pair = t * sec + c
            for j in range(wide.shape[0]):
                r, at = j // (width // LANES), j % (width // LANES) * LANES
                wide[j, pl.ds(pair, half, stride=terms * sec), :] = image[
                    r * half : (r + 1) * half, at : at + LANES
                ]
    for j in range(wide.shape[0]):
        out[:, j * LANES : (j + 1) * LANES] = wide[j].astype(BF16)


def order_kernel(left, right, conn, left_out, right_out, code):
    terms, classes, width = left.shape[0], left.shape[1], left.shape[2]
    nsec = conn.shape[1]
    order = split_order(width)
    code[...] = jnp.zeros_like(code)
    for t in range(terms):
        high = conn[t : t + 1, :] // CODE_BASE
        low = conn[t : t + 1, :] - high * CODE_BASE
        for j in range(nsec // width):
            code[pl.ds(j, 1), :] = high[:, j * width : (j + 1) * width].astype(F32)
            code[pl.ds(nsec // width + j, 1), :] = low[:, j * width : (j + 1) * width].astype(F32)
        left_out[t, classes * width :, :] = code[...].astype(BF16)
        for q in range(classes):
            left_out[t, q * width : (q + 1) * width, :] = matmul(order, left[t, q]).astype(BF16)
            right_out[t, q] = matmul_nt(right[t, q], order).astype(BF16)


def middle_kernel(classes, parts, qcol, *rest):
    sources, (out, wide) = rest[:-2], rest[-2:]
    each, nsec, width = sources[0].shape[0], parts.shape[1], sources[0].shape[2]
    terms = each * len(sources)
    half = width // 2
    total = parts[0].astype(F32)
    for x in range(1, parts.shape[0]):
        total = total + parts[x].astype(F32)
    for j in range(total.shape[1] // LANES):
        wide[4, pl.ds(j, nsec, stride=terms), :] = total[:, j * LANES : (j + 1) * LANES]
    for j in range(total.shape[1] // LANES, terms):
        wide[4, pl.ds(j, nsec, stride=terms), :] = jnp.zeros((nsec, LANES), F32)
    chosen = []
    for q in range(classes):
        kept = jnp.where(qcol[...] == q, total, 0.0).astype(BF16)
        chosen.append(jnp.concatenate([kept[:, :width], kept[:, width:]], axis=0))
    for t in range(terms):
        left = sources[t // each]
        image = matmul_nt(left[t % each, 0:width, :], chosen[0])
        for q in range(1, classes):
            image = image + matmul_nt(left[t % each, q * width : (q + 1) * width, :], chosen[q])
        for j in range(4):
            ri, r = j // 2, j % 2
            wide[j, pl.ds(t, half, stride=terms), :] = image[
                ri * half : (ri + 1) * half, r * nsec : (r + 1) * nsec
            ]
    for j in range(5):
        out[:, j * LANES : (j + 1) * LANES] = wide[j].astype(BF16)


def target_kernel(spread, moved, conn, qrow, dims, *rest):
    sources, (out, wide, images, route, sector) = rest[:-5], rest[-5:]
    each, classes, width = sources[0].shape[0], sources[0].shape[1], sources[0].shape[2]
    terms = each * len(sources)
    half, nsec = width // 2, conn.shape[1]
    blk, x = lax.axis_index("blk"), lax.axis_index("term")
    for j in range(5):
        wide[j] = moved[:, j * LANES : (j + 1) * LANES].astype(F32)
    for ih in range(2):
        for r in range(2):
            sector[ih, pl.ds(r, half, stride=2), :] = wide[4, pl.ds(2 * r + ih, half, stride=terms), :]
    source = iota((LANES, nsec), 0) * spread + x
    for t in range(terms):
        route[t * LANES : (t + 1) * LANES, :] = (conn[t : t + 1, :] == source).astype(F32).astype(BF16)
    classes_row = jnp.broadcast_to(qrow[...].astype(F32), (8, nsec)).astype(BF16)
    target = matmul_nt(classes_row, route[...])
    for t in range(terms):
        right = sources[t // each]
        both = jnp.concatenate(
            [
                jnp.concatenate(
                    [wide[2 * ri + r, pl.ds(t, half, stride=terms), :] for r in range(2)], axis=0
                )
                for ri in range(2)
            ],
            axis=1,
        ).astype(BF16)
        pick = target[0:1, t * LANES : (t + 1) * LANES]
        pick = jnp.concatenate([pick, pick], axis=1)
        image = matmul(right[t % each, 0], both)
        for q in range(1, classes):
            image = jnp.where(pick == float(q), matmul(right[t % each, q], both), image)
        high = image.astype(BF16)
        low = (image - high.astype(F32)).astype(BF16)
        for ri in range(2):
            at = slice(t * LANES, (t + 1) * LANES)
            images[0, ri * width : (ri + 1) * width, at] = high[:, ri * LANES : (ri + 1) * LANES]
            images[1, ri * width : (ri + 1) * width, at] = low[:, ri * LANES : (ri + 1) * LANES]
    total = matmul(images[0], route[...]) + matmul(images[1], route[...])
    line = iota((2 * width, 1), 0)
    ri = (line >= width).astype(jnp.int32)
    edge = jnp.maximum(2 * blk + ri, line - ri * width)
    total = jnp.where(edge < dims[...], total, 0.0).astype(BF16)
    turned = [sector[ih].T.astype(BF16) for ih in range(2)]
    each = nsec // out.shape[0]
    for to in range(out.shape[0]):
        out[to, : 2 * width, :] = total[:, to * each : (to + 1) * each]
        for lh in range(2):
            for ih in range(2):
                first = 2 * width + lh * width + ih * LANES
                out[to, first : first + LANES, :] = turned[ih][:, lh * LANES : (lh + 1) * LANES]


def last_kernel(parts, one, two):
    width = one.shape[1]
    total = parts[0, : 2 * width, :].astype(F32)
    for x in range(1, parts.shape[0]):
        total = total + parts[x, : 2 * width, :].astype(F32)
    two[...] = total.T.astype(BF16)
    for x in range(parts.shape[0]):
        for lh in range(2):
            one[x, :, lh * LANES : (lh + 1) * LANES] = parts[
                x, (2 + lh) * width : (3 + lh) * width, :
            ]


def call(kernel, out_shape, in_specs, scratch, vmem_bytes, flops, *operands):
    vmem = pl.BlockSpec(memory_space=pltpu.VMEM)
    return pl.pallas_call(
        kernel,
        out_shape=out_shape,
        in_specs=in_specs,
        out_specs=jax.tree.map(lambda _: vmem, out_shape),
        scratch_shapes=scratch,
        compiler_params=pltpu.CompilerParams(vmem_limit_bytes=vmem_bytes),
        cost_estimate=pl.CostEstimate(flops=flops, bytes_accessed=6 << 20, transcendentals=0),
    )(*operands)


def from_all(a, axis):
    n = lax.axis_size(axis)
    return [a] + [lax.ppermute(a, axis, [(i, (i + d) % n) for i in range(n)]) for d in range(1, n)]


def on_device(psi, left_env, right_env, connect, qclass, sector_dims):
    nblk = lax.axis_size("blk")
    nterm = lax.axis_size("term")
    sec, width = psi.shape[0], psi.shape[1]
    band = width // nblk
    nsec = qclass.shape[0]
    terms, classes = left_env.shape[0], left_env.shape[1]
    pairs = terms * sec
    kept = nsec // nterm
    all_terms = terms * nterm
    blk = lax.axis_index("blk")
    x = lax.axis_index("term")
    vmem = pl.BlockSpec(memory_space=pltpu.VMEM)
    hbm = pl.BlockSpec(memory_space=pl.ANY)
    bf16 = lambda *shape: jax.ShapeDtypeStruct(shape, BF16)
    q_row, d_row = qclass[None, :], sector_dims[None, :]

    def by_owner(a):
        return a.reshape(nblk, sec).T.reshape(nsec)

    sent = call(
        source_kernel,
        bf16(nblk * pairs, band * width),
        [hbm] * 6,
        [
            pltpu.VMEM(psi.shape, BF16),
            pltpu.VMEM(left_env.shape, BF16),
            pltpu.VMEM(right_env.shape, BF16),
            pltpu.VMEM(connect.shape, jnp.int32),
            pltpu.VMEM(q_row.shape, jnp.int32),
            pltpu.SMEM(q_row.shape, jnp.int32),
            pltpu.SMEM(d_row.shape, jnp.int32),
            pltpu.VMEM(right_env.shape, F32),
            pltpu.VMEM((band * width // LANES, nblk * pairs, LANES), F32),
            pltpu.SemaphoreType.DMA((7,)),
        ],
        None,
        (2 * pairs + terms * classes) * 2 * width**3,
        psi, left_env, right_env, connect, q_row, d_row,
    )
    left_mine, right_mine = call(
        order_kernel,
        (
            bf16(terms, classes * width + CODE_ROWS, width),
            bf16(terms, classes, width, width),
        ),
        [vmem] * 3,
        [pltpu.VMEM((CODE_ROWS, width), F32)],
        8 << 20,
        2 * terms * classes * 2 * width**3,
        left_env, right_env, connect,
    )
    lefts = from_all(left_mine, "term")
    rights = from_all(right_mine, "term")
    code = jnp.concatenate([a[:, classes * width :, :] for a in lefts], axis=0).astype(F32)
    halves = nsec // width
    conn_all = CODE_BASE * code[:, :halves].reshape(all_terms, nsec) + code[
        :, halves : 2 * halves
    ].reshape(all_terms, nsec)
    conn_all = conn_all.astype(jnp.int32)

    k = jnp.arange(nblk * pairs, dtype=jnp.int32)
    k_term = (k // sec) % terms
    k_sector = (k // pairs) * sec + k % sec
    wanted = jnp.zeros((nsec, k.shape[0]), jnp.int32)
    for t in range(terms):
        wanted = jnp.where(k_term[None, :] == t, by_owner(connect[t])[:, None], wanted)
    route = (wanted == k_sector[None, :]).astype(BF16)
    element = jnp.arange(band * width, dtype=jnp.int32)
    edge = jnp.maximum(blk * band + element // width, element % width)
    keep = edge[None, :] < by_owner(sector_dims)[:, None]
    qcol = lax.dynamic_slice_in_dim(by_owner(qclass), x * kept, kept)[:, None]

    moved = lax.all_to_all(
        sent.reshape(nblk, pairs, band * width), "blk", split_axis=0, concat_axis=0, tiled=True
    ).reshape(nblk * pairs, band * width)
    total = jnp.where(keep, matmul(route, moved), 0.0).astype(BF16)
    parts = lax.all_to_all(
        total.reshape(nterm, kept, band * width), "term", split_axis=0, concat_axis=0, tiled=True
    )
    sent = call(
        functools.partial(middle_kernel, classes),
        bf16(nblk * all_terms, band * width + LANES),
        [vmem] * (2 + nterm),
        [pltpu.VMEM((5, nblk * all_terms, LANES), F32)],
        16 << 20,
        2 * all_terms * classes * width**3,
        parts, qcol, *lefts,
    )
    sent, rights, conn_all = lax.optimization_barrier((sent, rights, conn_all))
    moved = lax.all_to_all(
        sent.reshape(nblk, all_terms, -1), "blk", split_axis=0, concat_axis=0, tiled=True
    ).reshape(nblk * all_terms, -1)
    sent = call(
        functools.partial(target_kernel, sec),
        bf16(nterm, 4 * width, kept),
        [vmem] * (4 + nterm),
        [
            pltpu.VMEM((5, nblk * all_terms, LANES), F32),
            pltpu.VMEM((2, band * width, all_terms * LANES), BF16),
            pltpu.VMEM((all_terms * LANES, nsec), BF16),
            pltpu.VMEM((2, width, LANES), F32),
        ],
        24 << 20,
        2 * all_terms * (classes * width**3 + 2 * 2 * width * LANES * nsec),
        moved, conn_all, q_row, d_row, *rights,
    )
    parts = lax.all_to_all(sent, "term", split_axis=0, concat_axis=0, tiled=True)
    sigma_one, two = call(
        last_kernel,
        (bf16(sec, width, width), bf16(kept, band * width)),
        [vmem],
        [],
        16 << 20,
        0,
        parts,
    )
    return (sigma_one, two.reshape(kept, band, width))


def solution(mesh):
    placed = (
        P("blk", None, None),
        P("term", None, None, None),
        P("term", None, None, None),
        P("term", None),
        P(),
        P(),
    )
    return jax.shard_map(
        on_device,
        mesh=mesh,
        in_specs=placed,
        out_specs=(P("blk", None, None), P("term", "blk", None)),
        check_vma=False,
    )
```

```python
import functools

import jax
import jax.numpy as jnp
from jax import lax
from jax.experimental import pallas as pl
from jax.experimental.pallas import tpu as pltpu
from jax.sharding import PartitionSpec as P

LANES = 128
ROWS = 4
CODE_ROWS = 16
CODE_BASE = 16
F32, BF16 = jnp.float32, jnp.bfloat16
NT = (((1,), (1,)), ((), ()))


def matmul(a, b):
    return jnp.dot(a, b, preferred_element_type=F32)


def matmul_nt(a, b):
    return lax.dot_general(a, b, NT, preferred_element_type=F32)


def iota(shape, dim):
    return lax.broadcasted_iota(jnp.int32, shape, dim)


def split_order(width):
    half = width // 2
    line = iota((width, width), 0)
    place = jnp.where(line < half, 2 * line, 2 * line - width + 1)
    return (place == iota((width, width), 1)).astype(F32).astype(BF16)


def source_kernel(
    psi_hbm, left_hbm, right_hbm, conn_hbm, qclass_hbm, dims_hbm,
    out,
    psi, left, right, conn, qrow, qclass, dims, right_rows, wide, sems,
):
    sec, width = psi.shape[0], psi.shape[1]
    terms, classes = left.shape[0], left.shape[1]
    half = width // 2
    pairs = (
        (right_hbm, right), (conn_hbm, conn), (left_hbm, left),
        (qclass_hbm, qclass), (qclass_hbm, qrow), (dims_hbm, dims), (psi_hbm, psi),
    )
    copies = [pltpu.make_async_copy(a, b, sems.at[i]) for i, (a, b) in enumerate(pairs)]
    for copy in copies:
        copy.start()
    order = split_order(width)
    edge = jnp.maximum(iota((width, width), 0), iota((width, width), 1))
    first = lax.axis_index("blk") * sec
    copies[0].wait()
    for t in range(terms):
        for q in range(classes):
            right_rows[t, q] = matmul(order, right[t, q])
    for copy in copies[1:]:
        copy.wait()
    for c in range(sec):
        own = first + c
        masked = jnp.where(edge < dims[0, own], psi[c].astype(F32), 0.0).astype(BF16)
        target = jnp.sum(jnp.where(conn[...] == own, qrow[...].astype(F32), 0.0), axis=1, keepdims=True)
        for t in range(terms):
            contracted = matmul(left[t, qclass[0, own]], masked).astype(BF16)
            chosen = right_rows[t, 0]
            for q in range(1, classes):
                chosen = jnp.where(target[t : t + 1, :] == float(q), right_rows[t, q], chosen)
            image = matmul_nt(chosen.astype(BF16), contracted)
            pair = t * sec + c
            for j in range(wide.shape[0]):
                r, at = j // (width // LANES), j % (width // LANES) * LANES
                wide[j, pl.ds(pair, half, stride=terms * sec), :] = image[
                    r * half : (r + 1) * half, at : at + LANES
                ]
    for j in range(wide.shape[0]):
        out[:, j * LANES : (j + 1) * LANES] = wide[j].astype(BF16)


def order_kernel(left, right, conn, left_out, right_out, code):
    terms, classes, width = left.shape[0], left.shape[1], left.shape[2]
    nsec = conn.shape[1]
    order = split_order(width)
    code[...] = jnp.zeros_like(code)
    for t in range(terms):
        high = conn[t : t + 1, :] // CODE_BASE
        low = conn[t : t + 1, :] - high * CODE_BASE
        for j in range(nsec // width):
            code[pl.ds(j, 1), :] = high[:, j * width : (j + 1) * width].astype(F32)
            code[pl.ds(nsec // width + j, 1), :] = low[:, j * width : (j + 1) * width].astype(F32)
        left_out[t, classes * width :, :] = code[...].astype(BF16)
        for q in range(classes):
            left_out[t, q * width : (q + 1) * width, :] = matmul(order, left[t, q]).astype(BF16)
            right_out[t, q] = matmul_nt(right[t, q], order).astype(BF16)


def middle_kernel(classes, parts, qcol, *rest):
    sources, (out, wide) = rest[:-2], rest[-2:]
    each, nsec, width = sources[0].shape[0], parts.shape[1], sources[0].shape[2]
    terms = each * len(sources)
    half = width // 2
    total = parts[0].astype(F32)
    for x in range(1, parts.shape[0]):
        total = total + parts[x].astype(F32)
    for j in range(ROWS):
        wide[wide.shape[0] - 1, pl.ds(j, nsec, stride=ROWS), :] = total[:, j * LANES : (j + 1) * LANES]
    chosen = []
    for q in range(classes):
        kept = jnp.where(qcol[...] == q, total, 0.0).astype(BF16)
        chosen.append(jnp.concatenate([kept[:, :width], kept[:, width:]], axis=0))
    for t in range(terms):
        left = sources[t // each]
        image = matmul_nt(left[t % each, 0:width, :], chosen[0])
        for q in range(1, classes):
            image = image + matmul_nt(left[t % each, q * width : (q + 1) * width, :], chosen[q])
        for j in range(4):
            ri, r = j // 2, j % 2
            wide[4 * (t // ROWS) + j, pl.ds(t % ROWS, half, stride=ROWS), :] = image[
                ri * half : (ri + 1) * half, r * nsec : (r + 1) * nsec
            ]
    for j in range(wide.shape[0]):
        out[:, :, j * LANES : (j + 1) * LANES] = wide[j].reshape(half, ROWS, LANES).astype(BF16)


def target_kernel(spread, moved, conn, qrow, dims, *rest):
    sources, (out, wide, images, route, sector) = rest[:-5], rest[-5:]
    each, classes, width = sources[0].shape[0], sources[0].shape[1], sources[0].shape[2]
    terms = each * len(sources)
    half, nsec = width // 2, conn.shape[1]
    blk, x = lax.axis_index("blk"), lax.axis_index("term")
    for j in range(wide.shape[0]):
        wide[j] = moved[:, :, j * LANES : (j + 1) * LANES].astype(F32).reshape(half * ROWS, LANES)
    for ih in range(2):
        for r in range(2):
            sector[ih, pl.ds(r, half, stride=2), :] = wide[wide.shape[0] - 1, pl.ds(2 * r + ih, half, stride=ROWS), :]
    source = iota((LANES, nsec), 0) * spread + x
    for t in range(terms):
        route[t * LANES : (t + 1) * LANES, :] = (conn[t : t + 1, :] == source).astype(F32).astype(BF16)
    classes_row = jnp.broadcast_to(qrow[...].astype(F32), (8, nsec)).astype(BF16)
    target = matmul_nt(classes_row, route[...])
    for t in range(terms):
        right = sources[t // each]
        both = jnp.concatenate(
            [
                jnp.concatenate(
                    [
                        wide[4 * (t // ROWS) + 2 * ri + r, pl.ds(t % ROWS, half, stride=ROWS), :]
                        for r in range(2)
                    ],
                    axis=0,
                )
                for ri in range(2)
            ],
            axis=1,
        ).astype(BF16)
        pick = target[0:1, t * LANES : (t + 1) * LANES]
        pick = jnp.concatenate([pick, pick], axis=1)
        image = matmul(right[t % each, 0], both)
        for q in range(1, classes):
            image = jnp.where(pick == float(q), matmul(right[t % each, q], both), image)
        high = image.astype(BF16)
        low = (image - high.astype(F32)).astype(BF16)
        for ri in range(2):
            at = slice(t * LANES, (t + 1) * LANES)
            images[0, ri * width : (ri + 1) * width, at] = high[:, ri * LANES : (ri + 1) * LANES]
            images[1, ri * width : (ri + 1) * width, at] = low[:, ri * LANES : (ri + 1) * LANES]
    total = matmul(images[0], route[...]) + matmul(images[1], route[...])
    line = iota((2 * width, 1), 0)
    ri = (line >= width).astype(jnp.int32)
    edge = jnp.maximum(2 * blk + ri, line - ri * width)
    total = jnp.where(edge < dims[...], total, 0.0).astype(BF16)
    turned = [sector[ih].T.astype(BF16) for ih in range(2)]
    each = nsec // out.shape[0]
    for to in range(out.shape[0]):
        out[to, : 2 * width, :] = total[:, to * each : (to + 1) * each]
        for lh in range(2):
            for ih in range(2):
                first = 2 * width + lh * width + ih * LANES
                out[to, first : first + LANES, :] = turned[ih][:, lh * LANES : (lh + 1) * LANES]


def last_kernel(parts, one, two, rows):
    width = one.shape[1]
    total = parts[0, : 2 * width, :].astype(F32)
    for x in range(1, parts.shape[0]):
        total = total + parts[x, : 2 * width, :].astype(F32)
    total = total.T
    kept = total.shape[0]
    for j in range(2 * width // LANES):
        ri, at = j // (width // LANES), j % (width // LANES)
        rows[at, pl.ds(ri, kept, stride=2), :] = total[:, j * LANES : (j + 1) * LANES]
    for at in range(width // LANES):
        two[:, :, at * LANES : (at + 1) * LANES] = rows[at].reshape(kept, 2, LANES).astype(BF16)
    for x in range(parts.shape[0]):
        for lh in range(2):
            one[x, :, lh * LANES : (lh + 1) * LANES] = parts[
                x, (2 + lh) * width : (3 + lh) * width, :
            ]


def call(kernel, out_shape, in_specs, scratch, vmem_bytes, flops, *operands):
    vmem = pl.BlockSpec(memory_space=pltpu.VMEM)
    return pl.pallas_call(
        kernel,
        out_shape=out_shape,
        in_specs=in_specs,
        out_specs=jax.tree.map(lambda _: vmem, out_shape),
        scratch_shapes=scratch,
        compiler_params=pltpu.CompilerParams(vmem_limit_bytes=vmem_bytes),
        cost_estimate=pl.CostEstimate(flops=flops, bytes_accessed=6 << 20, transcendentals=0),
    )(*operands)


def from_all(a, axis):
    n = lax.axis_size(axis)
    return [a] + [lax.ppermute(a, axis, [(i, (i + d) % n) for i in range(n)]) for d in range(1, n)]


def on_device(psi, left_env, right_env, connect, qclass, sector_dims):
    nblk = lax.axis_size("blk")
    nterm = lax.axis_size("term")
    sec, width = psi.shape[0], psi.shape[1]
    band = width // nblk
    nsec = qclass.shape[0]
    terms, classes = left_env.shape[0], left_env.shape[1]
    pairs = terms * sec
    kept = nsec // nterm
    all_terms = terms * nterm
    slots = all_terms // ROWS * band * band + 1
    blk = lax.axis_index("blk")
    x = lax.axis_index("term")
    vmem = pl.BlockSpec(memory_space=pltpu.VMEM)
    hbm = pl.BlockSpec(memory_space=pl.ANY)
    bf16 = lambda *shape: jax.ShapeDtypeStruct(shape, BF16)
    q_row, d_row = qclass[None, :], sector_dims[None, :]

    def by_owner(a):
        return a.reshape(nblk, sec).T.reshape(nsec)

    sent = call(
        source_kernel,
        bf16(nblk * pairs, band * width),
        [hbm] * 6,
        [
            pltpu.VMEM(psi.shape, BF16),
            pltpu.VMEM(left_env.shape, BF16),
            pltpu.VMEM(right_env.shape, BF16),
            pltpu.VMEM(connect.shape, jnp.int32),
            pltpu.VMEM(q_row.shape, jnp.int32),
            pltpu.SMEM(q_row.shape, jnp.int32),
            pltpu.SMEM(d_row.shape, jnp.int32),
            pltpu.VMEM(right_env.shape, F32),
            pltpu.VMEM((band * width // LANES, nblk * pairs, LANES), F32),
            pltpu.SemaphoreType.DMA((7,)),
        ],
        None,
        (2 * pairs + terms * classes) * 2 * width**3,
        psi, left_env, right_env, connect, q_row, d_row,
    )
    left_mine, right_mine = call(
        order_kernel,
        (
            bf16(terms, classes * width + CODE_ROWS, width),
            bf16(terms, classes, width, width),
        ),
        [vmem] * 3,
        [pltpu.VMEM((CODE_ROWS, width), F32)],
        8 << 20,
        2 * terms * classes * 2 * width**3,
        left_env, right_env, connect,
    )
    lefts = from_all(left_mine, "term")
    rights = from_all(right_mine, "term")
    code = jnp.concatenate([a[:, classes * width :, :] for a in lefts], axis=0).astype(F32)
    halves = nsec // width
    conn_all = CODE_BASE * code[:, :halves].reshape(all_terms, nsec) + code[
        :, halves : 2 * halves
    ].reshape(all_terms, nsec)
    conn_all = conn_all.astype(jnp.int32)

    k = jnp.arange(nblk * pairs, dtype=jnp.int32)
    k_term = (k // sec) % terms
    k_sector = (k // pairs) * sec + k % sec
    wanted = jnp.zeros((nsec, k.shape[0]), jnp.int32)
    for t in range(terms):
        wanted = jnp.where(k_term[None, :] == t, by_owner(connect[t])[:, None], wanted)
    route = (wanted == k_sector[None, :]).astype(BF16)
    element = jnp.arange(band * width, dtype=jnp.int32)
    edge = jnp.maximum(blk * band + element // width, element % width)
    keep = edge[None, :] < by_owner(sector_dims)[:, None]
    qcol = lax.dynamic_slice_in_dim(by_owner(qclass), x * kept, kept)[:, None]

    moved = lax.all_to_all(
        sent.reshape(nblk, pairs, band * width), "blk", split_axis=0, concat_axis=0, tiled=True
    ).reshape(nblk * pairs, band * width)
    total = jnp.where(keep, matmul(route, moved), 0.0).astype(BF16)
    parts = lax.all_to_all(
        total.reshape(nterm, kept, band * width), "term", split_axis=0, concat_axis=0, tiled=True
    )
    sent = call(
        functools.partial(middle_kernel, classes),
        bf16(nblk, ROWS, slots * LANES),
        [vmem] * (2 + nterm),
        [pltpu.VMEM((slots, nblk * ROWS, LANES), F32)],
        16 << 20,
        2 * all_terms * classes * width**3,
        parts, qcol, *lefts,
    )
    sent, rights, conn_all = lax.optimization_barrier((sent, rights, conn_all))
    moved = lax.all_to_all(sent, "blk", split_axis=0, concat_axis=0, tiled=True)
    sent = call(
        functools.partial(target_kernel, sec),
        bf16(nterm, 4 * width, kept),
        [vmem] * (4 + nterm),
        [
            pltpu.VMEM((slots, nblk * ROWS, LANES), F32),
            pltpu.VMEM((2, band * width, all_terms * LANES), BF16),
            pltpu.VMEM((all_terms * LANES, nsec), BF16),
            pltpu.VMEM((2, width, LANES), F32),
        ],
        24 << 20,
        2 * all_terms * (classes * width**3 + 2 * 2 * width * LANES * nsec),
        moved, conn_all, q_row, d_row, *rights,
    )
    parts = lax.all_to_all(sent, "term", split_axis=0, concat_axis=0, tiled=True)
    sigma_one, two = call(
        last_kernel,
        (bf16(sec, width, width), bf16(kept, band, width)),
        [vmem],
        [pltpu.VMEM((width // LANES, kept * band, LANES), F32)],
        16 << 20,
        0,
        parts,
    )
    return (sigma_one, two)


def solution(mesh):
    placed = (
        P("blk", None, None),
        P("term", None, None, None),
        P("term", None, None, None),
        P("term", None),
        P(),
        P(),
    )
    return jax.shard_map(
        on_device,
        mesh=mesh,
        in_specs=placed,
        out_specs=(P("blk", None, None), P("term", "blk", None)),
        check_vma=False,
    )
```

```python
import functools

import jax
import jax.numpy as jnp
from jax import lax
from jax.experimental import pallas as pl
from jax.experimental.pallas import tpu as pltpu
from jax.sharding import PartitionSpec as P

LANES = 128
ROWS = 4
CODE_ROWS = 16
CODE_BASE = 16
F32, BF16 = jnp.float32, jnp.bfloat16
NT = (((1,), (1,)), ((), ()))


def matmul(a, b):
    return jnp.dot(a, b, preferred_element_type=F32)


def matmul_nt(a, b):
    return lax.dot_general(a, b, NT, preferred_element_type=F32)


def iota(shape, dim):
    return lax.broadcasted_iota(jnp.int32, shape, dim)


def split_order(width):
    half = width // 2
    line = iota((width, width), 0)
    place = jnp.where(line < half, 2 * line, 2 * line - width + 1)
    return (place == iota((width, width), 1)).astype(F32).astype(BF16)


def source_kernel(
    psi_hbm, left_hbm, right_hbm, conn_hbm, qclass_hbm, dims_hbm,
    out,
    psi, left, right, conn, qrow, qclass, dims, right_rows, wide, sems,
):
    sec, width = psi.shape[0], psi.shape[1]
    terms, classes = left.shape[0], left.shape[1]
    half = width // 2
    pairs = (
        (right_hbm, right), (conn_hbm, conn), (left_hbm, left),
        (qclass_hbm, qclass), (qclass_hbm, qrow), (dims_hbm, dims), (psi_hbm, psi),
    )
    copies = [pltpu.make_async_copy(a, b, sems.at[i]) for i, (a, b) in enumerate(pairs)]
    for copy in copies:
        copy.start()
    order = split_order(width)
    edge = jnp.maximum(iota((width, width), 0), iota((width, width), 1))
    first = lax.axis_index("blk") * sec
    copies[0].wait()
    for t in range(terms):
        for q in range(classes):
            right_rows[t, q] = matmul(order, right[t, q])
    for copy in copies[1:]:
        copy.wait()
    for c in range(sec):
        own = first + c
        masked = jnp.where(edge < dims[0, own], psi[c].astype(F32), 0.0).astype(BF16)
        target = jnp.sum(jnp.where(conn[...] == own, qrow[...].astype(F32), 0.0), axis=1, keepdims=True)
        for t in range(terms):
            contracted = matmul(left[t, qclass[0, own]], masked).astype(BF16)
            chosen = right_rows[t, 0]
            for q in range(1, classes):
                chosen = jnp.where(target[t : t + 1, :] == float(q), right_rows[t, q], chosen)
            image = matmul_nt(chosen.astype(BF16), contracted)
            pair = t * sec + c
            for j in range(wide.shape[0]):
                r, at = j // (width // LANES), j % (width // LANES) * LANES
                wide[j, pl.ds(pair, half, stride=terms * sec), :] = image[
                    r * half : (r + 1) * half, at : at + LANES
                ]
    for j in range(wide.shape[0]):
        out[:, j * LANES : (j + 1) * LANES] = wide[j].astype(BF16)


def order_kernel(left, right, conn, left_out, right_out, code):
    terms, classes, width = left.shape[0], left.shape[1], left.shape[2]
    nsec = conn.shape[1]
    order = split_order(width)
    code[...] = jnp.zeros_like(code)
    for t in range(terms):
        high = conn[t : t + 1, :] // CODE_BASE
        low = conn[t : t + 1, :] - high * CODE_BASE
        for j in range(nsec // width):
            code[pl.ds(j, 1), :] = high[:, j * width : (j + 1) * width].astype(F32)
            code[pl.ds(nsec // width + j, 1), :] = low[:, j * width : (j + 1) * width].astype(F32)
        left_out[t, classes * width :, :] = code[...].astype(BF16)
        for q in range(classes):
            left_out[t, q * width : (q + 1) * width, :] = matmul(order, left[t, q]).astype(BF16)
            right_out[t, q] = matmul_nt(right[t, q], order).astype(BF16)


def middle_kernel(classes, parts, qcol, *rest):
    sources, (out, wide) = rest[:-2], rest[-2:]
    each, nsec, width = sources[0].shape[0], parts.shape[1], sources[0].shape[2]
    terms = each * len(sources)
    half = width // 2
    total = parts[0].astype(F32)
    for x in range(1, parts.shape[0]):
        total = total + parts[x].astype(F32)
    for j in range(ROWS):
        wide[wide.shape[0] - 1, pl.ds(j, nsec, stride=ROWS), :] = total[:, j * LANES : (j + 1) * LANES]
    chosen = []
    for q in range(classes):
        kept = jnp.where(qcol[...] == q, total, 0.0).astype(BF16)
        chosen.append(jnp.concatenate([kept[:, :width], kept[:, width:]], axis=0))
    for t in range(terms):
        left = sources[t // each]
        image = matmul_nt(left[t % each, 0:width, :], chosen[0])
        for q in range(1, classes):
            image = image + matmul_nt(left[t % each, q * width : (q + 1) * width, :], chosen[q])
        for j in range(4):
            ri, r = j // 2, j % 2
            wide[4 * (t // ROWS) + j, pl.ds(t % ROWS, half, stride=ROWS), :] = image[
                ri * half : (ri + 1) * half, r * nsec : (r + 1) * nsec
            ]
    for j in range(wide.shape[0]):
        out[:, :, j * LANES : (j + 1) * LANES] = wide[j].reshape(half, ROWS, LANES).astype(BF16)


def target_kernel(spread, moved, conn, qrow, dims, *rest):
    sources, (out, wide, images, route, sector) = rest[:-5], rest[-5:]
    each, classes, width = sources[0].shape[0], sources[0].shape[1], sources[0].shape[2]
    terms = each * len(sources)
    half, nsec = width // 2, conn.shape[1]
    blk, x = lax.axis_index("blk"), lax.axis_index("term")
    for j in range(wide.shape[0]):
        wide[j] = moved[:, :, j * LANES : (j + 1) * LANES].astype(F32).reshape(half * ROWS, LANES)
    for ih in range(2):
        for r in range(2):
            sector[ih, pl.ds(r, half, stride=2), :] = wide[wide.shape[0] - 1, pl.ds(2 * r + ih, half, stride=ROWS), :]
    source = iota((LANES, nsec), 0) * spread + x
    for t in range(terms):
        route[t * LANES : (t + 1) * LANES, :] = (conn[t : t + 1, :] == source).astype(F32).astype(BF16)
    classes_row = jnp.broadcast_to(qrow[...].astype(F32), (8, nsec)).astype(BF16)
    target = matmul_nt(classes_row, route[...])
    for t in range(terms):
        right = sources[t // each]
        both = jnp.concatenate(
            [
                jnp.concatenate(
                    [
                        wide[4 * (t // ROWS) + 2 * ri + r, pl.ds(t % ROWS, half, stride=ROWS), :]
                        for r in range(2)
                    ],
                    axis=0,
                )
                for ri in range(2)
            ],
            axis=1,
        ).astype(BF16)
        pick = target[0:1, t * LANES : (t + 1) * LANES]
        pick = jnp.concatenate([pick, pick], axis=1)
        image = matmul(right[t % each, 0], both)
        for q in range(1, classes):
            image = jnp.where(pick == float(q), matmul(right[t % each, q], both), image)
        high = image.astype(BF16)
        low = (image - high.astype(F32)).astype(BF16)
        for ri in range(2):
            at = slice(t * LANES, (t + 1) * LANES)
            images[0, ri * width : (ri + 1) * width, at] = high[:, ri * LANES : (ri + 1) * LANES]
            images[1, ri * width : (ri + 1) * width, at] = low[:, ri * LANES : (ri + 1) * LANES]
    total = matmul(images[0], route[...]) + matmul(images[1], route[...])
    line = iota((2 * width, 1), 0)
    ri = (line >= width).astype(jnp.int32)
    edge = jnp.maximum(2 * blk + ri, line - ri * width)
    total = jnp.where(edge < dims[...], total, 0.0).astype(BF16)
    turned = [sector[ih].T.astype(BF16) for ih in range(2)]
    each = nsec // out.shape[0]
    for to in range(out.shape[0]):
        out[to, : 2 * width, :] = total[:, to * each : (to + 1) * each]
        for lh in range(2):
            for ih in range(2):
                first = 2 * width + lh * width + ih * LANES
                out[to, first : first + LANES, :] = turned[ih][:, lh * LANES : (lh + 1) * LANES]


def last_kernel(parts, one, two, rows):
    width = one.shape[1]
    total = parts[0, : 2 * width, :].astype(F32)
    for x in range(1, parts.shape[0]):
        total = total + parts[x, : 2 * width, :].astype(F32)
    total = total.T
    kept = total.shape[0]
    for j in range(2 * width // LANES):
        ri, at = j // (width // LANES), j % (width // LANES)
        rows[at, pl.ds(ri, kept, stride=2), :] = total[:, j * LANES : (j + 1) * LANES]
    for at in range(width // LANES):
        two[:, :, at * LANES : (at + 1) * LANES] = rows[at].reshape(kept, 2, LANES).astype(BF16)
    for x in range(parts.shape[0]):
        for lh in range(2):
            one[x, :, lh * LANES : (lh + 1) * LANES] = parts[
                x, (2 + lh) * width : (3 + lh) * width, :
            ]


def call(kernel, out_shape, in_specs, scratch, vmem_bytes, flops, *operands):
    vmem = pl.BlockSpec(memory_space=pltpu.VMEM)
    return pl.pallas_call(
        kernel,
        out_shape=out_shape,
        in_specs=in_specs,
        out_specs=jax.tree.map(lambda _: vmem, out_shape),
        scratch_shapes=scratch,
        compiler_params=pltpu.CompilerParams(vmem_limit_bytes=vmem_bytes),
        cost_estimate=pl.CostEstimate(flops=flops, bytes_accessed=6 << 20, transcendentals=0),
    )(*operands)


def from_all(a, axis, way):
    n = lax.axis_size(axis)
    step = lambda v, d: lax.ppermute(v, axis, [(i, (i + d) % n) for i in range(n)])
    slots = {0: a, 1: step(a, 1), n - 1: step(a, -1)}
    for d in range(2, n - 1):
        slots[d] = step(slots[(d - way) % n], way)
    return [slots[d] for d in range(n)]


def on_device(psi, left_env, right_env, connect, qclass, sector_dims):
    nblk = lax.axis_size("blk")
    nterm = lax.axis_size("term")
    sec, width = psi.shape[0], psi.shape[1]
    band = width // nblk
    nsec = qclass.shape[0]
    terms, classes = left_env.shape[0], left_env.shape[1]
    pairs = terms * sec
    kept = nsec // nterm
    all_terms = terms * nterm
    slots = all_terms // ROWS * band * band + 1
    blk = lax.axis_index("blk")
    x = lax.axis_index("term")
    vmem = pl.BlockSpec(memory_space=pltpu.VMEM)
    hbm = pl.BlockSpec(memory_space=pl.ANY)
    bf16 = lambda *shape: jax.ShapeDtypeStruct(shape, BF16)
    q_row, d_row = qclass[None, :], sector_dims[None, :]

    def by_owner(a):
        return a.reshape(nblk, sec).T.reshape(nsec)

    sent = call(
        source_kernel,
        bf16(nblk * pairs, band * width),
        [hbm] * 6,
        [
            pltpu.VMEM(psi.shape, BF16),
            pltpu.VMEM(left_env.shape, BF16),
            pltpu.VMEM(right_env.shape, BF16),
            pltpu.VMEM(connect.shape, jnp.int32),
            pltpu.VMEM(q_row.shape, jnp.int32),
            pltpu.SMEM(q_row.shape, jnp.int32),
            pltpu.SMEM(d_row.shape, jnp.int32),
            pltpu.VMEM(right_env.shape, F32),
            pltpu.VMEM((band * width // LANES, nblk * pairs, LANES), F32),
            pltpu.SemaphoreType.DMA((7,)),
        ],
        None,
        (2 * pairs + terms * classes) * 2 * width**3,
        psi, left_env, right_env, connect, q_row, d_row,
    )
    left_mine, right_mine = call(
        order_kernel,
        (
            bf16(terms, classes * width + CODE_ROWS, width),
            bf16(terms, classes, width, width),
        ),
        [vmem] * 3,
        [pltpu.VMEM((CODE_ROWS, width), F32)],
        8 << 20,
        2 * terms * classes * 2 * width**3,
        left_env, right_env, connect,
    )
    lefts = from_all(left_mine, "term", 1)
    rights = from_all(right_mine, "term", -1)
    code = jnp.concatenate([a[:, classes * width :, :] for a in lefts], axis=0).astype(F32)
    halves = nsec // width
    conn_all = CODE_BASE * code[:, :halves].reshape(all_terms, nsec) + code[
        :, halves : 2 * halves
    ].reshape(all_terms, nsec)
    conn_all = conn_all.astype(jnp.int32)

    k = jnp.arange(nblk * pairs, dtype=jnp.int32)
    k_term = (k // sec) % terms
    k_sector = (k // pairs) * sec + k % sec
    wanted = jnp.zeros((nsec, k.shape[0]), jnp.int32)
    for t in range(terms):
        wanted = jnp.where(k_term[None, :] == t, by_owner(connect[t])[:, None], wanted)
    route = (wanted == k_sector[None, :]).astype(BF16)
    element = jnp.arange(band * width, dtype=jnp.int32)
    edge = jnp.maximum(blk * band + element // width, element % width)
    keep = edge[None, :] < by_owner(sector_dims)[:, None]
    qcol = lax.dynamic_slice_in_dim(by_owner(qclass), x * kept, kept)[:, None]

    moved = lax.all_to_all(
        sent.reshape(nblk, pairs, band * width), "blk", split_axis=0, concat_axis=0, tiled=True
    ).reshape(nblk * pairs, band * width)
    total = jnp.where(keep, matmul(route, moved), 0.0).astype(BF16)
    parts = lax.all_to_all(
        total.reshape(nterm, kept, band * width), "term", split_axis=0, concat_axis=0, tiled=True
    )
    sent = call(
        functools.partial(middle_kernel, classes),
        bf16(nblk, ROWS, slots * LANES),
        [vmem] * (2 + nterm),
        [pltpu.VMEM((slots, nblk * ROWS, LANES), F32)],
        16 << 20,
        2 * all_terms * classes * width**3,
        parts, qcol, *lefts,
    )
    sent, rights, conn_all = lax.optimization_barrier((sent, rights, conn_all))
    moved = lax.all_to_all(sent, "blk", split_axis=0, concat_axis=0, tiled=True)
    sent = call(
        functools.partial(target_kernel, sec),
        bf16(nterm, 4 * width, kept),
        [vmem] * (4 + nterm),
        [
            pltpu.VMEM((slots, nblk * ROWS, LANES), F32),
            pltpu.VMEM((2, band * width, all_terms * LANES), BF16),
            pltpu.VMEM((all_terms * LANES, nsec), BF16),
            pltpu.VMEM((2, width, LANES), F32),
        ],
        24 << 20,
        2 * all_terms * (classes * width**3 + 2 * 2 * width * LANES * nsec),
        moved, conn_all, q_row, d_row, *rights,
    )
    parts = lax.all_to_all(sent, "term", split_axis=0, concat_axis=0, tiled=True)
    sigma_one, two = call(
        last_kernel,
        (bf16(sec, width, width), bf16(kept, band, width)),
        [vmem],
        [pltpu.VMEM((width // LANES, kept * band, LANES), F32)],
        16 << 20,
        0,
        parts,
    )
    return (sigma_one, two)


def solution(mesh):
    placed = (
        P("blk", None, None),
        P("term", None, None, None),
        P("term", None, None, None),
        P("term", None),
        P(),
        P(),
    )
    return jax.shard_map(
        on_device,
        mesh=mesh,
        in_specs=placed,
        out_specs=(P("blk", None, None), P("term", "blk", None)),
        check_vma=False,
    )
```

```python
import functools

import jax
import jax.numpy as jnp
from jax import lax
from jax.experimental import pallas as pl
from jax.experimental.pallas import tpu as pltpu
from jax.sharding import PartitionSpec as P

LANES = 128
ROWS = 4
CODE_ROWS = 16
CODE_BASE = 16
F32, BF16 = jnp.float32, jnp.bfloat16
NT = (((1,), (1,)), ((), ()))


def matmul(a, b):
    return jnp.dot(a, b, preferred_element_type=F32)


def matmul_nt(a, b):
    return lax.dot_general(a, b, NT, preferred_element_type=F32)


def iota(shape, dim):
    return lax.broadcasted_iota(jnp.int32, shape, dim)


def split_order(width):
    half = width // 2
    line = iota((width, width), 0)
    place = jnp.where(line < half, 2 * line, 2 * line - width + 1)
    return (place == iota((width, width), 1)).astype(F32).astype(BF16)


def source_kernel(
    psi_hbm, left_hbm, right_hbm, conn_hbm, qclass_hbm, dims_hbm,
    out,
    psi, left, right, conn, qrow, qclass, dims, right_rows, wide, sems,
):
    sec, width = psi.shape[0], psi.shape[1]
    terms, classes = left.shape[0], left.shape[1]
    half = width // 2
    pairs = (
        (right_hbm, right), (conn_hbm, conn), (left_hbm, left),
        (qclass_hbm, qclass), (qclass_hbm, qrow), (dims_hbm, dims), (psi_hbm, psi),
    )
    copies = [pltpu.make_async_copy(a, b, sems.at[i]) for i, (a, b) in enumerate(pairs)]
    for copy in copies:
        copy.start()
    order = split_order(width)
    edge = jnp.maximum(iota((width, width), 0), iota((width, width), 1))
    first = lax.axis_index("blk") * sec
    copies[0].wait()
    for t in range(terms):
        for q in range(classes):
            right_rows[t, q] = matmul(order, right[t, q])
    for copy in copies[1:]:
        copy.wait()
    for c in range(sec):
        own = first + c
        masked = jnp.where(edge < dims[0, own], psi[c].astype(F32), 0.0).astype(BF16)
        target = jnp.sum(jnp.where(conn[...] == own, qrow[...].astype(F32), 0.0), axis=1, keepdims=True)
        for t in range(terms):
            contracted = matmul(left[t, qclass[0, own]], masked).astype(BF16)
            chosen = right_rows[t, 0]
            for q in range(1, classes):
                chosen = jnp.where(target[t : t + 1, :] == float(q), right_rows[t, q], chosen)
            image = matmul_nt(chosen.astype(BF16), contracted)
            pair = t * sec + c
            for j in range(wide.shape[0]):
                r, at = j // (width // LANES), j % (width // LANES) * LANES
                wide[j, pl.ds(pair, half, stride=terms * sec), :] = image[
                    r * half : (r + 1) * half, at : at + LANES
                ]
    for j in range(wide.shape[0]):
        out[:, j * LANES : (j + 1) * LANES] = wide[j].astype(BF16)


def order_kernel(left, right, conn, left_out, right_out, code):
    terms, classes, width = left.shape[0], left.shape[1], left.shape[2]
    nsec = conn.shape[1]
    order = split_order(width)
    code[...] = jnp.zeros_like(code)
    for t in range(terms):
        high = conn[t : t + 1, :] // CODE_BASE
        low = conn[t : t + 1, :] - high * CODE_BASE
        for j in range(nsec // width):
            code[pl.ds(j, 1), :] = high[:, j * width : (j + 1) * width].astype(F32)
            code[pl.ds(nsec // width + j, 1), :] = low[:, j * width : (j + 1) * width].astype(F32)
        left_out[t, classes * width :, :] = code[...].astype(BF16)
        for q in range(classes):
            left_out[t, q * width : (q + 1) * width, :] = matmul(order, left[t, q]).astype(BF16)
            right_out[t, q] = matmul_nt(right[t, q], order).astype(BF16)


def sum_kernel(sec, terms, moved_hbm, rows_in, out, moved, route, sems):
    parts = sems.shape[0]
    deep = moved.shape[0] // parts
    copies = []
    for i in range(parts):
        rows = pl.ds(i * deep, deep)
        copies.append(pltpu.make_async_copy(moved_hbm.at[rows], moved.at[rows], sems.at[i]))
        copies[-1].start()
    cols = rows_in[...].astype(F32).T
    width = out.shape[1] // 2
    k = iota((1, route.shape[1]), 1)
    which = (k // sec) % terms
    sector = (k // (terms * sec)) * sec + k % sec
    wanted = jnp.broadcast_to(cols[:, 0:1], route.shape)
    for t in range(1, terms):
        wanted = jnp.where(which == t, cols[:, t : t + 1], wanted)
    route[...] = (wanted == sector.astype(F32)).astype(F32).astype(BF16)
    total = None
    for i in range(parts):
        copies[i].wait()
        at = slice(i * deep, (i + 1) * deep)
        image = matmul(route[:, at], moved[at, :])
        total = image if total is None else total + image
    line = iota((1, out.shape[1]), 1)
    r = (line >= width).astype(jnp.int32)
    edge = jnp.maximum(2 * lax.axis_index("blk") + r, line - r * width)
    out[...] = jnp.where(edge.astype(F32) < cols[:, terms : terms + 1], total, 0.0).astype(BF16)


def middle_kernel(classes, spread, parts, qrow, *rest):
    sources, (out, wide) = rest[:-2], rest[-2:]
    each, nsec, width = sources[0].shape[0], parts.shape[1], sources[0].shape[2]
    terms = each * len(sources)
    half = width // 2
    total = parts[0].astype(F32)
    for x in range(1, parts.shape[0]):
        total = total + parts[x].astype(F32)
    for j in range(ROWS):
        wide[wide.shape[0] - 1, pl.ds(j, nsec, stride=ROWS), :] = total[:, j * LANES : (j + 1) * LANES]
    kept = total.astype(BF16)
    stacked = jnp.concatenate([kept[:, :width], kept[:, width:]], axis=0)
    mine = iota((nsec, qrow.shape[1]), 0) * spread + lax.axis_index("term")
    mine = (mine == iota((nsec, qrow.shape[1]), 1)).astype(F32).astype(BF16)
    classes_row = jnp.broadcast_to(qrow[...].astype(F32), (8, qrow.shape[1])).astype(BF16)
    pick = matmul_nt(classes_row, mine)[0:1, :]
    pick = jnp.concatenate([pick, pick], axis=1)
    for t in range(terms):
        left = sources[t // each]
        image = matmul_nt(left[t % each, 0:width, :], stacked)
        for q in range(1, classes):
            other = matmul_nt(left[t % each, q * width : (q + 1) * width, :], stacked)
            image = jnp.where(pick == float(q), other, image)
        for j in range(4):
            ri, r = j // 2, j % 2
            wide[4 * (t // ROWS) + j, pl.ds(t % ROWS, half, stride=ROWS), :] = image[
                ri * half : (ri + 1) * half, r * nsec : (r + 1) * nsec
            ]
    for j in range(wide.shape[0]):
        out[:, :, j * LANES : (j + 1) * LANES] = wide[j].reshape(half, ROWS, LANES).astype(BF16)


def target_kernel(spread, moved, conn, qrow, dims, *rest):
    sources, (out, wide, images, route, sector) = rest[:-5], rest[-5:]
    each, classes, width = sources[0].shape[0], sources[0].shape[1], sources[0].shape[2]
    terms = each * len(sources)
    half, nsec = width // 2, conn.shape[1]
    blk, x = lax.axis_index("blk"), lax.axis_index("term")
    for j in range(wide.shape[0]):
        wide[j] = moved[:, :, j * LANES : (j + 1) * LANES].astype(F32).reshape(half * ROWS, LANES)
    for ih in range(2):
        for r in range(2):
            sector[ih, pl.ds(r, half, stride=2), :] = wide[wide.shape[0] - 1, pl.ds(2 * r + ih, half, stride=ROWS), :]
    source = iota((LANES, nsec), 0) * spread + x
    for t in range(terms):
        route[t * LANES : (t + 1) * LANES, :] = (conn[t : t + 1, :] == source).astype(F32).astype(BF16)
    classes_row = jnp.broadcast_to(qrow[...].astype(F32), (8, nsec)).astype(BF16)
    target = matmul_nt(classes_row, route[...])
    for t in range(terms):
        right = sources[t // each]
        both = jnp.concatenate(
            [
                jnp.concatenate(
                    [
                        wide[4 * (t // ROWS) + 2 * ri + r, pl.ds(t % ROWS, half, stride=ROWS), :]
                        for r in range(2)
                    ],
                    axis=0,
                )
                for ri in range(2)
            ],
            axis=1,
        ).astype(BF16)
        pick = target[0:1, t * LANES : (t + 1) * LANES]
        pick = jnp.concatenate([pick, pick], axis=1)
        image = matmul(right[t % each, 0], both)
        for q in range(1, classes):
            image = jnp.where(pick == float(q), matmul(right[t % each, q], both), image)
        high = image.astype(BF16)
        low = (image - high.astype(F32)).astype(BF16)
        for ri in range(2):
            at = slice(t * LANES, (t + 1) * LANES)
            images[0, ri * width : (ri + 1) * width, at] = high[:, ri * LANES : (ri + 1) * LANES]
            images[1, ri * width : (ri + 1) * width, at] = low[:, ri * LANES : (ri + 1) * LANES]
    total = matmul(images[0], route[...]) + matmul(images[1], route[...])
    line = iota((2 * width, 1), 0)
    ri = (line >= width).astype(jnp.int32)
    edge = jnp.maximum(2 * blk + ri, line - ri * width)
    total = jnp.where(edge < dims[...], total, 0.0).astype(BF16)
    turned = [sector[ih].T.astype(BF16) for ih in range(2)]
    each = nsec // out.shape[0]
    for to in range(out.shape[0]):
        out[to, : 2 * width, :] = total[:, to * each : (to + 1) * each]
        for lh in range(2):
            for ih in range(2):
                first = 2 * width + lh * width + ih * LANES
                out[to, first : first + LANES, :] = turned[ih][:, lh * LANES : (lh + 1) * LANES]


def last_kernel(parts, one, two, rows):
    width = one.shape[1]
    total = parts[0, : 2 * width, :].astype(F32)
    for x in range(1, parts.shape[0]):
        total = total + parts[x, : 2 * width, :].astype(F32)
    total = total.T
    kept = total.shape[0]
    for j in range(2 * width // LANES):
        ri, at = j // (width // LANES), j % (width // LANES)
        rows[at, pl.ds(ri, kept, stride=2), :] = total[:, j * LANES : (j + 1) * LANES]
    for at in range(width // LANES):
        two[:, :, at * LANES : (at + 1) * LANES] = rows[at].reshape(kept, 2, LANES).astype(BF16)
    for x in range(parts.shape[0]):
        for lh in range(2):
            one[x, :, lh * LANES : (lh + 1) * LANES] = parts[
                x, (2 + lh) * width : (3 + lh) * width, :
            ]


def call(kernel, out_shape, in_specs, scratch, vmem_bytes, flops, *operands):
    vmem = pl.BlockSpec(memory_space=pltpu.VMEM)
    return pl.pallas_call(
        kernel,
        out_shape=out_shape,
        in_specs=in_specs,
        out_specs=jax.tree.map(lambda _: vmem, out_shape),
        scratch_shapes=scratch,
        compiler_params=pltpu.CompilerParams(vmem_limit_bytes=vmem_bytes),
        cost_estimate=pl.CostEstimate(flops=flops, bytes_accessed=6 << 20, transcendentals=0),
    )(*operands)


def from_all(a, axis, way):
    n = lax.axis_size(axis)
    step = lambda v, d: lax.ppermute(v, axis, [(i, (i + d) % n) for i in range(n)])
    slots = {0: a, 1: step(a, 1), n - 1: step(a, -1)}
    for d in range(2, n - 1):
        slots[d] = step(slots[(d - way) % n], way)
    return [slots[d] for d in range(n)]


def on_device(psi, left_env, right_env, connect, qclass, sector_dims):
    nblk = lax.axis_size("blk")
    nterm = lax.axis_size("term")
    sec, width = psi.shape[0], psi.shape[1]
    band = width // nblk
    nsec = qclass.shape[0]
    terms, classes = left_env.shape[0], left_env.shape[1]
    pairs = terms * sec
    kept = nsec // nterm
    all_terms = terms * nterm
    slots = all_terms // ROWS * band * band + 1
    blk = lax.axis_index("blk")
    x = lax.axis_index("term")
    vmem = pl.BlockSpec(memory_space=pltpu.VMEM)
    hbm = pl.BlockSpec(memory_space=pl.ANY)
    bf16 = lambda *shape: jax.ShapeDtypeStruct(shape, BF16)
    q_row, d_row = qclass[None, :], sector_dims[None, :]

    def by_owner(a):
        return a.reshape(nblk, sec).T.reshape(nsec)

    sent = call(
        source_kernel,
        bf16(nblk * pairs, band * width),
        [hbm] * 6,
        [
            pltpu.VMEM(psi.shape, BF16),
            pltpu.VMEM(left_env.shape, BF16),
            pltpu.VMEM(right_env.shape, BF16),
            pltpu.VMEM(connect.shape, jnp.int32),
            pltpu.VMEM(q_row.shape, jnp.int32),
            pltpu.SMEM(q_row.shape, jnp.int32),
            pltpu.SMEM(d_row.shape, jnp.int32),
            pltpu.VMEM(right_env.shape, F32),
            pltpu.VMEM((band * width // LANES, nblk * pairs, LANES), F32),
            pltpu.SemaphoreType.DMA((7,)),
        ],
        None,
        (2 * pairs + terms * classes) * 2 * width**3,
        psi, left_env, right_env, connect, q_row, d_row,
    )
    left_mine, right_mine = call(
        order_kernel,
        (
            bf16(terms, classes * width + CODE_ROWS, width),
            bf16(terms, classes, width, width),
        ),
        [vmem] * 3,
        [pltpu.VMEM((CODE_ROWS, width), F32)],
        8 << 20,
        2 * terms * classes * 2 * width**3,
        left_env, right_env, connect,
    )
    lefts = from_all(left_mine, "term", 1)
    rights = from_all(right_mine, "term", -1)
    code = jnp.concatenate([a[:, classes * width :, :] for a in lefts], axis=0).astype(F32)
    halves = nsec // width
    conn_all = CODE_BASE * code[:, :halves].reshape(all_terms, nsec) + code[
        :, halves : 2 * halves
    ].reshape(all_terms, nsec)
    conn_all = conn_all.astype(jnp.int32)

    rows = jnp.stack([by_owner(connect[t]) for t in range(terms)] + [by_owner(sector_dims)])
    rows = jnp.pad(rows, ((0, -rows.shape[0] % 8), (0, 0)))
    moved = lax.all_to_all(
        sent.reshape(nblk, pairs, band * width), "blk", split_axis=0, concat_axis=0, tiled=True
    ).reshape(nblk * pairs, band * width)
    moved, lefts, rights, conn_all = lax.optimization_barrier((moved, lefts, rights, conn_all))
    total = call(
        functools.partial(sum_kernel, sec, terms),
        bf16(nsec, band * width),
        [hbm, vmem],
        [
            pltpu.VMEM((nblk * pairs, band * width), BF16),
            pltpu.VMEM((nsec, nblk * pairs), BF16),
            pltpu.SemaphoreType.DMA((2,)),
        ],
        12 << 20,
        2 * nsec * nblk * pairs * band * width,
        moved, rows,
    )
    parts = lax.all_to_all(
        total.reshape(nterm, kept, band * width), "term", split_axis=0, concat_axis=0, tiled=True
    )
    sent = call(
        functools.partial(middle_kernel, classes, sec),
        bf16(nblk, ROWS, slots * LANES),
        [vmem] * (2 + nterm),
        [pltpu.VMEM((slots, nblk * ROWS, LANES), F32)],
        16 << 20,
        2 * all_terms * classes * width**3,
        parts, q_row, *lefts,
    )
    moved = lax.all_to_all(sent, "blk", split_axis=0, concat_axis=0, tiled=True)
    sent = call(
        functools.partial(target_kernel, sec),
        bf16(nterm, 4 * width, kept),
        [vmem] * (4 + nterm),
        [
            pltpu.VMEM((slots, nblk * ROWS, LANES), F32),
            pltpu.VMEM((2, band * width, all_terms * LANES), BF16),
            pltpu.VMEM((all_terms * LANES, nsec), BF16),
            pltpu.VMEM((2, width, LANES), F32),
        ],
        24 << 20,
        2 * all_terms * (classes * width**3 + 2 * 2 * width * LANES * nsec),
        moved, conn_all, q_row, d_row, *rights,
    )
    parts = lax.all_to_all(sent, "term", split_axis=0, concat_axis=0, tiled=True)
    sigma_one, two = call(
        last_kernel,
        (bf16(sec, width, width), bf16(kept, band, width)),
        [vmem],
        [pltpu.VMEM((width // LANES, kept * band, LANES), F32)],
        16 << 20,
        0,
        parts,
    )
    return (sigma_one, two)


def solution(mesh):
    placed = (
        P("blk", None, None),
        P("term", None, None, None),
        P("term", None, None, None),
        P("term", None),
        P(),
        P(),
    )
    return jax.shard_map(
        on_device,
        mesh=mesh,
        in_specs=placed,
        out_specs=(P("blk", None, None), P("term", "blk", None)),
        check_vma=False,
    )
```

```python
import functools

import jax
import jax.numpy as jnp
from jax import lax
from jax.experimental import pallas as pl
from jax.experimental.pallas import tpu as pltpu
from jax.sharding import PartitionSpec as P

LANES = 128
ROWS = 4
CODE_ROWS = 16
CODE_BASE = 16
F32, BF16 = jnp.float32, jnp.bfloat16
NT = (((1,), (1,)), ((), ()))


def matmul(a, b):
    return jnp.dot(a, b, preferred_element_type=F32)


def matmul_nt(a, b):
    return lax.dot_general(a, b, NT, preferred_element_type=F32)


def iota(shape, dim):
    return lax.broadcasted_iota(jnp.int32, shape, dim)


def split_order(width):
    half = width // 2
    line = iota((width, width), 0)
    place = jnp.where(line < half, 2 * line, 2 * line - width + 1)
    return (place == iota((width, width), 1)).astype(F32).astype(BF16)


def source_kernel(
    psi_hbm, left_hbm, right_hbm, conn_hbm, qclass_hbm, dims_hbm,
    out,
    psi, left, right, conn, qrow, qclass, dims, right_rows, wide, sems,
):
    sec, width = psi.shape[0], psi.shape[1]
    terms, classes = left.shape[0], left.shape[1]
    half = width // 2
    pairs = (
        (right_hbm, right), (conn_hbm, conn), (left_hbm, left),
        (qclass_hbm, qclass), (qclass_hbm, qrow), (dims_hbm, dims), (psi_hbm, psi),
    )
    copies = [pltpu.make_async_copy(a, b, sems.at[i]) for i, (a, b) in enumerate(pairs)]
    for copy in copies:
        copy.start()
    order = split_order(width)
    edge = jnp.maximum(iota((width, width), 0), iota((width, width), 1))
    first = lax.axis_index("blk") * sec
    copies[0].wait()
    for t in range(terms):
        for q in range(classes):
            right_rows[t, q] = matmul(order, right[t, q])
    for copy in copies[1:]:
        copy.wait()
    for c in range(sec):
        own = first + c
        masked = jnp.where(edge < dims[0, own], psi[c].astype(F32), 0.0).astype(BF16)
        target = jnp.sum(jnp.where(conn[...] == own, qrow[...].astype(F32), 0.0), axis=1, keepdims=True)
        for t in range(terms):
            contracted = matmul(left[t, qclass[0, own]], masked).astype(BF16)
            chosen = right_rows[t, 0]
            for q in range(1, classes):
                chosen = jnp.where(target[t : t + 1, :] == float(q), right_rows[t, q], chosen)
            image = matmul_nt(chosen.astype(BF16), contracted)
            pair = t * sec + c
            for j in range(wide.shape[0]):
                r, at = j // (width // LANES), j % (width // LANES) * LANES
                wide[j, pl.ds(pair, half, stride=terms * sec), :] = image[
                    r * half : (r + 1) * half, at : at + LANES
                ]
    for j in range(wide.shape[0]):
        out[:, j * LANES : (j + 1) * LANES] = wide[j].astype(BF16)


def order_kernel(left, right, conn, left_out, right_out, code):
    terms, classes, width = left.shape[0], left.shape[1], left.shape[2]
    nsec = conn.shape[1]
    order = split_order(width)
    code[...] = jnp.zeros_like(code)
    for t in range(terms):
        high = conn[t : t + 1, :] // CODE_BASE
        low = conn[t : t + 1, :] - high * CODE_BASE
        for j in range(nsec // width):
            code[pl.ds(j, 1), :] = high[:, j * width : (j + 1) * width].astype(F32)
            code[pl.ds(nsec // width + j, 1), :] = low[:, j * width : (j + 1) * width].astype(F32)
        left_out[t, classes * width :, :] = code[...].astype(BF16)
        for q in range(classes):
            left_out[t, q * width : (q + 1) * width, :] = matmul(order, left[t, q]).astype(BF16)
            right_out[t, q] = matmul_nt(right[t, q], order).astype(BF16)


def middle_kernel(classes, spread, parts, qrow, *rest):
    sources, (out, wide) = rest[:-2], rest[-2:]
    each, nsec, width = sources[0].shape[0], parts.shape[1], sources[0].shape[2]
    terms = each * len(sources)
    half = width // 2
    total = parts[0].astype(F32)
    for x in range(1, parts.shape[0]):
        total = total + parts[x].astype(F32)
    for j in range(ROWS):
        wide[wide.shape[0] - 1, pl.ds(j, nsec, stride=ROWS), :] = total[:, j * LANES : (j + 1) * LANES]
    kept = total.astype(BF16)
    stacked = jnp.concatenate([kept[:, :width], kept[:, width:]], axis=0)
    mine = iota((nsec, qrow.shape[1]), 0) * spread + lax.axis_index("term")
    mine = (mine == iota((nsec, qrow.shape[1]), 1)).astype(F32).astype(BF16)
    classes_row = jnp.broadcast_to(qrow[...].astype(F32), (8, qrow.shape[1])).astype(BF16)
    pick = matmul_nt(classes_row, mine)[0:1, :]
    pick = jnp.concatenate([pick, pick], axis=1)
    for t in range(terms):
        left = sources[t // each]
        image = matmul_nt(left[t % each, 0:width, :], stacked)
        for q in range(1, classes):
            other = matmul_nt(left[t % each, q * width : (q + 1) * width, :], stacked)
            image = jnp.where(pick == float(q), other, image)
        for j in range(4):
            ri, r = j // 2, j % 2
            wide[4 * (t // ROWS) + j, pl.ds(t % ROWS, half, stride=ROWS), :] = image[
                ri * half : (ri + 1) * half, r * nsec : (r + 1) * nsec
            ]
    for j in range(wide.shape[0]):
        out[:, :, j * LANES : (j + 1) * LANES] = wide[j].reshape(half, ROWS, LANES).astype(BF16)


def target_kernel(spread, moved, conn, qrow, dims, *rest):
    sources, (out, wide, images, route, sector) = rest[:-5], rest[-5:]
    each, classes, width = sources[0].shape[0], sources[0].shape[1], sources[0].shape[2]
    terms = each * len(sources)
    half, nsec = width // 2, conn.shape[1]
    blk, x = lax.axis_index("blk"), lax.axis_index("term")
    for j in range(wide.shape[0]):
        wide[j] = moved[:, :, j * LANES : (j + 1) * LANES].astype(F32).reshape(half * ROWS, LANES)
    for ih in range(2):
        for r in range(2):
            sector[ih, pl.ds(r, half, stride=2), :] = wide[wide.shape[0] - 1, pl.ds(2 * r + ih, half, stride=ROWS), :]
    source = iota((LANES, nsec), 0) * spread + x
    for t in range(terms):
        route[t * LANES : (t + 1) * LANES, :] = (conn[t : t + 1, :] == source).astype(F32).astype(BF16)
    classes_row = jnp.broadcast_to(qrow[...].astype(F32), (8, nsec)).astype(BF16)
    target = matmul_nt(classes_row, route[...])
    for t in range(terms):
        right = sources[t // each]
        both = jnp.concatenate(
            [
                jnp.concatenate(
                    [
                        wide[4 * (t // ROWS) + 2 * ri + r, pl.ds(t % ROWS, half, stride=ROWS), :]
                        for r in range(2)
                    ],
                    axis=0,
                )
                for ri in range(2)
            ],
            axis=1,
        ).astype(BF16)
        pick = target[0:1, t * LANES : (t + 1) * LANES]
        pick = jnp.concatenate([pick, pick], axis=1)
        image = matmul(right[t % each, 0], both)
        for q in range(1, classes):
            image = jnp.where(pick == float(q), matmul(right[t % each, q], both), image)
        high = image.astype(BF16)
        low = (image - high.astype(F32)).astype(BF16)
        for ri in range(2):
            at = slice(t * LANES, (t + 1) * LANES)
            images[0, ri * width : (ri + 1) * width, at] = high[:, ri * LANES : (ri + 1) * LANES]
            images[1, ri * width : (ri + 1) * width, at] = low[:, ri * LANES : (ri + 1) * LANES]
    total = matmul(images[0], route[...]) + matmul(images[1], route[...])
    line = iota((2 * width, 1), 0)
    ri = (line >= width).astype(jnp.int32)
    edge = jnp.maximum(2 * blk + ri, line - ri * width)
    total = jnp.where(edge < dims[...], total, 0.0).astype(BF16)
    turned = [sector[ih].T.astype(BF16) for ih in range(2)]
    each = nsec // out.shape[0]
    for to in range(out.shape[0]):
        out[to, : 2 * width, :] = total[:, to * each : (to + 1) * each]
        for lh in range(2):
            for ih in range(2):
                first = 2 * width + lh * width + ih * LANES
                out[to, first : first + LANES, :] = turned[ih][:, lh * LANES : (lh + 1) * LANES]


def last_kernel(parts, one, two, rows):
    width = one.shape[1]
    total = parts[0, : 2 * width, :].astype(F32)
    for x in range(1, parts.shape[0]):
        total = total + parts[x, : 2 * width, :].astype(F32)
    total = total.T
    kept = total.shape[0]
    for j in range(2 * width // LANES):
        ri, at = j // (width // LANES), j % (width // LANES)
        rows[at, pl.ds(ri, kept, stride=2), :] = total[:, j * LANES : (j + 1) * LANES]
    for at in range(width // LANES):
        two[:, :, at * LANES : (at + 1) * LANES] = rows[at].reshape(kept, 2, LANES).astype(BF16)
    for x in range(parts.shape[0]):
        for lh in range(2):
            one[x, :, lh * LANES : (lh + 1) * LANES] = parts[
                x, (2 + lh) * width : (3 + lh) * width, :
            ]


def call(kernel, out_shape, in_specs, scratch, vmem_bytes, flops, *operands):
    vmem = pl.BlockSpec(memory_space=pltpu.VMEM)
    return pl.pallas_call(
        kernel,
        out_shape=out_shape,
        in_specs=in_specs,
        out_specs=jax.tree.map(lambda _: vmem, out_shape),
        scratch_shapes=scratch,
        compiler_params=pltpu.CompilerParams(vmem_limit_bytes=vmem_bytes),
        cost_estimate=pl.CostEstimate(flops=flops, bytes_accessed=6 << 20, transcendentals=0),
    )(*operands)


def from_all(a, axis, way):
    n = lax.axis_size(axis)
    step = lambda v, d: lax.ppermute(v, axis, [(i, (i + d) % n) for i in range(n)])
    slots = {0: a, 1: step(a, 1), n - 1: step(a, -1)}
    for d in range(2, n - 1):
        slots[d] = step(slots[(d - way) % n], way)
    return [slots[d] for d in range(n)]


def on_device(psi, left_env, right_env, connect, qclass, sector_dims):
    nblk = lax.axis_size("blk")
    nterm = lax.axis_size("term")
    sec, width = psi.shape[0], psi.shape[1]
    band = width // nblk
    nsec = qclass.shape[0]
    terms, classes = left_env.shape[0], left_env.shape[1]
    pairs = terms * sec
    kept = nsec // nterm
    all_terms = terms * nterm
    slots = all_terms // ROWS * band * band + 1
    blk = lax.axis_index("blk")
    x = lax.axis_index("term")
    vmem = pl.BlockSpec(memory_space=pltpu.VMEM)
    hbm = pl.BlockSpec(memory_space=pl.ANY)
    bf16 = lambda *shape: jax.ShapeDtypeStruct(shape, BF16)
    q_row, d_row = qclass[None, :], sector_dims[None, :]

    def by_owner(a):
        return a.reshape(nblk, sec).T.reshape(nsec)

    sent = call(
        source_kernel,
        bf16(nblk * pairs, band * width),
        [hbm] * 6,
        [
            pltpu.VMEM(psi.shape, BF16),
            pltpu.VMEM(left_env.shape, BF16),
            pltpu.VMEM(right_env.shape, BF16),
            pltpu.VMEM(connect.shape, jnp.int32),
            pltpu.VMEM(q_row.shape, jnp.int32),
            pltpu.SMEM(q_row.shape, jnp.int32),
            pltpu.SMEM(d_row.shape, jnp.int32),
            pltpu.VMEM(right_env.shape, F32),
            pltpu.VMEM((band * width // LANES, nblk * pairs, LANES), F32),
            pltpu.SemaphoreType.DMA((7,)),
        ],
        None,
        (2 * pairs + terms * classes) * 2 * width**3,
        psi, left_env, right_env, connect, q_row, d_row,
    )
    left_mine, right_mine = call(
        order_kernel,
        (
            bf16(terms, classes * width + CODE_ROWS, width),
            bf16(terms, classes, width, width),
        ),
        [vmem] * 3,
        [pltpu.VMEM((CODE_ROWS, width), F32)],
        8 << 20,
        2 * terms * classes * 2 * width**3,
        left_env, right_env, connect,
    )
    lefts = from_all(left_mine, "term", 1)
    rights = from_all(right_mine, "term", -1)
    code = jnp.concatenate([a[:, classes * width :, :] for a in lefts], axis=0).astype(F32)
    halves = nsec // width
    conn_all = CODE_BASE * code[:, :halves].reshape(all_terms, nsec) + code[
        :, halves : 2 * halves
    ].reshape(all_terms, nsec)
    conn_all = conn_all.astype(jnp.int32)

    k = jnp.arange(nblk * pairs, dtype=jnp.int32)
    k_term = (k // sec) % terms
    k_sector = (k // pairs) * sec + k % sec
    wanted = jnp.zeros((nsec, k.shape[0]), jnp.int32)
    for t in range(terms):
        wanted = jnp.where(k_term[None, :] == t, by_owner(connect[t])[:, None], wanted)
    route = (wanted == k_sector[None, :]).astype(BF16)
    element = jnp.arange(band * width, dtype=jnp.int32)
    edge = jnp.maximum(blk * band + element // width, element % width)
    keep = edge[None, :] < by_owner(sector_dims)[:, None]
    moved = lax.all_to_all(
        sent.reshape(nblk, pairs, band * width), "blk", split_axis=0, concat_axis=0, tiled=True
    ).reshape(nblk * pairs, band * width)
    moved, lefts, rights, conn_all = lax.optimization_barrier((moved, lefts, rights, conn_all))
    total = jnp.where(keep, matmul(route, moved), 0.0).astype(BF16)
    parts = lax.all_to_all(
        total.reshape(nterm, kept, band * width), "term", split_axis=0, concat_axis=0, tiled=True
    )
    sent = call(
        functools.partial(middle_kernel, classes, sec),
        bf16(nblk, ROWS, slots * LANES),
        [vmem] * (2 + nterm),
        [pltpu.VMEM((slots, nblk * ROWS, LANES), F32)],
        16 << 20,
        2 * all_terms * classes * width**3,
        parts, q_row, *lefts,
    )
    moved = lax.all_to_all(sent, "blk", split_axis=0, concat_axis=0, tiled=True)
    sent = call(
        functools.partial(target_kernel, sec),
        bf16(nterm, 4 * width, kept),
        [vmem] * (4 + nterm),
        [
            pltpu.VMEM((slots, nblk * ROWS, LANES), F32),
            pltpu.VMEM((2, band * width, all_terms * LANES), BF16),
            pltpu.VMEM((all_terms * LANES, nsec), BF16),
            pltpu.VMEM((2, width, LANES), F32),
        ],
        24 << 20,
        2 * all_terms * (classes * width**3 + 2 * 2 * width * LANES * nsec),
        moved, conn_all, q_row, d_row, *rights,
    )
    parts = lax.all_to_all(sent, "term", split_axis=0, concat_axis=0, tiled=True)
    sigma_one, two = call(
        last_kernel,
        (bf16(sec, width, width), bf16(kept, band, width)),
        [vmem],
        [pltpu.VMEM((width // LANES, kept * band, LANES), F32)],
        16 << 20,
        0,
        parts,
    )
    return (sigma_one, two)


def solution(mesh):
    placed = (
        P("blk", None, None),
        P("term", None, None, None),
        P("term", None, None, None),
        P("term", None),
        P(),
        P(),
    )
    return jax.shard_map(
        on_device,
        mesh=mesh,
        in_specs=placed,
        out_specs=(P("blk", None, None), P("term", "blk", None)),
        check_vma=False,
    )
```
